32 devices in a mesh: groups: 2 (over x), tm: 16 (over z, y, core).
Axes of the slice: x: 2, y: 2, z: 4, core: 2. Of those that a mesh axis runs over, the one named last changes fastest.
Arguments:
- token_ids: int32 [4096, 8], P(('groups', 'tm')), parts along dimension 0, may hold values from 0 to 127
- field_offsets: int32 [16], P('groups'), parts along dimension 0, may hold values from 0 to 896
- embed_table: bfloat16 [1024, 1024], replicated, may hold values from -2.09375 to 2.09375
- w_in: bfloat16 [1024, 3072], P('tm'), may hold values from -0.1875 to 0.1875
- short_taps: float32 [3, 3072], replicated, may hold values from -1 to 1
- filters: bfloat16 [2, 1024, 2048], P(None, 'tm'), may hold values from -1.1 to 1.1
- cotangent: bfloat16 [4096, 1024], P(('groups', 'tm')), parts along dimension 0, may hold values from -0.125 to 0.125
Outputs:
- mixer_out: bfloat16 [4096, 1024], P(('groups', 'tm')), parts along dimension 0
- weight_grads: float32 [2048, 3072], P(('groups', 'tm')), parts along dimension 0
- tap_grads: float32 [6, 3072], P('groups'), parts along dimension 0
- filter_grads: float32 [4, 1024, 2048], P('groups', 'tm'), parts along dimension 0
The draws below stay inside these ranges and needn't reach their ends.
There are 2 independent parts, one for each index of `groups`. The reference program is written for one: setup_inputs(seed, part) draws one part's arguments, and reference() takes and returns one part's arrays. A program takes and returns all parts, laid end to end along the dimension named above; an argument that names none is the same for every part. Nothing has to cross between parts.
All inputs are finite; a program needn't handle non-finite values.
Results may differ from the reference program's by a relative error of at most 0.035.
Values may be sent and summed in bfloat16 or wider, within the bound.
No kernel may reach another device: no remote copies, remote signals or barrier semaphores. Data moves between devices by JAX's collectives and lax.ppermute only.
A program may use at most 128 MiB of HBM per device.

```python
import jax
import jax.numpy as jnp

D = 1024
S = 8
K = 128
V = 1024
TOKENS = 2048


def draw_filters(key, part):
    key_rate, key_noise = jax.random.split(key)
    length = TOKENS
    low = jnp.log(0.25 / length)
    high = jnp.log(1.0 / 30.0)
    rate = jnp.exp(jax.random.uniform(key_rate, (2, D, 1), jnp.float32, low, high))
    lag = jnp.arange(length, dtype=jnp.float32)[None, None, :]
    envelope = jnp.sqrt(2.0 * rate) * jnp.exp(-rate * lag)
    noise = jnp.clip(jax.random.normal(key_noise, (2, D, length), jnp.float32), -4.0, 4.0)
    return (envelope * noise).astype(jnp.bfloat16)


def with_ends(array, stream_key, smallest, high):
    longest = array.shape.index(max(array.shape))
    spots = []
    for shift in (0, 1):
        where = [jax.random.randint(jax.random.fold_in(stream_key, axis), (), 0, length) for axis, length in enumerate(array.shape)]
        where[longest] = (where[longest] + shift) % array.shape[longest]
        spots.append(tuple(where))
    return array.at[spots[0]].set(smallest).at[spots[1]].set(high)


def levels(key, shape, cuts, smallest, largest):
    factor_of, own = 1.0, jax.random.fold_in(key, 6)
    for position, blocks in cuts:
        steps = jnp.exp(jax.random.uniform(jax.random.fold_in(own, position), (blocks,), jnp.float32, smallest / len(cuts), largest / len(cuts)))
        factor_of = factor_of * jnp.repeat(steps, shape[position] // blocks).reshape([-1 if axis == position else 1 for axis in range(len(shape))])
    return factor_of


def gaussian(rng, dims, width, limit, shards=(), kind=jnp.bfloat16):
    array = jax.random.normal(rng, dims, jnp.float32) * width
    if len(shards) > 0:
        array = levels(rng, dims, shards, -0.22, 0.18) * array
    return jnp.clip(array, min=-limit, max=limit).astype(kind)


def setup_inputs(seed: int = 0, part: int = 0) -> dict:
    splits = jax.random.split(jax.random.key(seed), 8)
    part_keys = jax.random.split(jax.random.fold_in(splits[7], part), 8)
    return {
        "token_ids": with_ends(jax.random.randint(part_keys[0], (TOKENS, S), 0, K), jax.random.fold_in(part_keys[0], 1), 0, K - 1).astype(jnp.int32),
        "field_offsets": with_ends(jax.random.randint(part_keys[1], (S,), 0, V - K + 1), jax.random.fold_in(part_keys[1], 1), 0, V - K).astype(jnp.int32),
        "embed_table": gaussian(splits[2], (V, D), 0.35, 2.09375),
        "w_in": gaussian(splits[3], (D, 3 * D), D ** -0.5, 0.1875, ((0, 16),)),
        "short_taps": jnp.clip(jax.random.uniform(splits[4], (3, 3 * D), jnp.float32, -1.0, 1.0), -1.0, 1.0),
        "filters": draw_filters(jax.random.fold_in(splits[7], 71), part),
        "cotangent": gaussian(part_keys[6], (TOKENS, D), (TOKENS ** -0.5), 0.125, ((0, 16),)),
    }


def reference(token_ids, field_offsets, embed_table, w_in, short_taps, filters, cotangent):
    row_index = (token_ids + field_offsets[None, :]).astype(jnp.int32)
    embedded = jnp.sum(jnp.take(embed_table, row_index, axis=0).astype(jnp.float32), axis=1).astype(jnp.bfloat16)
    proj = jnp.dot(embedded, w_in, preferred_element_type=jnp.float32).astype(jnp.bfloat16)
    length = proj.shape[0]
    total = 2 * length
    proj_wide = proj.astype(jnp.float32)
    padded = jnp.concatenate([jnp.zeros((2, proj.shape[1]), jnp.float32), proj_wide], axis=0)
    mixed = (short_taps[0] * padded[2:] + short_taps[1] * padded[1:length + 1] + short_taps[2] * padded[:length]).astype(jnp.bfloat16)
    values = mixed[:, :D].astype(jnp.float32)
    first_gate = mixed[:, D:2 * D].astype(jnp.float32)
    second_gate = mixed[:, 2 * D:].astype(jnp.float32)

    def spectrum(series):
        return jnp.fft.rfft(series.T, n=total, axis=-1)

    def signal(spec):
        return jnp.fft.irfft(spec, n=total, axis=-1)[:, :length]

    first_spec = jnp.fft.rfft(filters[0].astype(jnp.float32), n=total, axis=-1)
    second_spec = jnp.fft.rfft(filters[1].astype(jnp.float32), n=total, axis=-1)
    value_spec = spectrum(values)
    first_conv = signal(value_spec * first_spec).T.astype(jnp.bfloat16).astype(jnp.float32)
    first_mix = (first_gate * first_conv).astype(jnp.bfloat16).astype(jnp.float32)
    mix_spec = spectrum(first_mix)
    second_conv = signal(mix_spec * second_spec).T.astype(jnp.bfloat16).astype(jnp.float32)
    mixer_out = (second_gate * second_conv).astype(jnp.bfloat16)
    upstream = cotangent.astype(jnp.float32)
    grad_conv2 = (upstream * second_gate).astype(jnp.bfloat16).astype(jnp.float32)
    grad_gate2 = (upstream * second_conv).astype(jnp.bfloat16)
    grad_spec2 = spectrum(grad_conv2)
    grad_mix = signal(grad_spec2 * jnp.conj(second_spec)).T.astype(jnp.bfloat16).astype(jnp.float32)
    filter_two = signal(grad_spec2 * jnp.conj(mix_spec))
    grad_gate1 = (grad_mix * first_conv).astype(jnp.bfloat16)
    grad_conv1 = (grad_mix * first_gate).astype(jnp.bfloat16).astype(jnp.float32)
    grad_spec1 = spectrum(grad_conv1)
    grad_values = signal(grad_spec1 * jnp.conj(first_spec)).T.astype(jnp.bfloat16)
    filter_one = signal(grad_spec1 * jnp.conj(value_spec))
    filter_grads = jnp.stack([filter_one, filter_two], axis=0)
    grad_mixed = jnp.concatenate([grad_values, grad_gate1, grad_gate2], axis=1).astype(jnp.float32)
    grad_padded = jnp.concatenate([grad_mixed, jnp.zeros((2, grad_mixed.shape[1]), jnp.float32)], axis=0)
    grad_proj = (short_taps[0] * grad_mixed + short_taps[1] * grad_padded[1:length + 1] + short_taps[2] * grad_padded[2:]).astype(jnp.bfloat16)
    tap_grads = jnp.stack([
        jnp.sum(grad_mixed * padded[2:], axis=0),
        jnp.sum(grad_mixed * padded[1:length + 1], axis=0),
        jnp.sum(grad_mixed * padded[:length], axis=0)], axis=0)
    weight_grads = jnp.dot(embedded.T, grad_proj, preferred_element_type=jnp.float32)
    return mixer_out, weight_grads, tap_grads, filter_grads
```

```python
import math

import jax
import jax.numpy as jnp
from jax import lax
from jax.sharding import PartitionSpec as P

HIGHEST = lax.Precision.HIGHEST


def cis_tables(count_a, count_b, modulus):
    left = jnp.arange(count_a, dtype=jnp.int32)[:, None]
    right = jnp.arange(count_b, dtype=jnp.int32)[None, :]
    angle = 2.0 * math.pi / modulus * (left * right % modulus).astype(jnp.float32)
    return (jnp.cos(angle), jnp.sin(angle))


def build_tables(first_len, second_len, total):
    first_cos, first_sin = cis_tables(first_len, first_len // 2, first_len)
    twist_cos, twist_sin = cis_tables(first_len, second_len, total)
    second_cos, second_sin = cis_tables(second_len, second_len, second_len)
    first_both = jnp.concatenate([first_cos, -first_sin], axis=0)
    forward_second = jnp.concatenate(
        [
            jnp.concatenate([second_cos, -second_sin], axis=1),
            jnp.concatenate([second_sin, second_cos], axis=1),
        ],
        axis=0,
    )
    inverse_second = jnp.concatenate(
        [
            jnp.concatenate([second_cos, second_sin], axis=1),
            jnp.concatenate([-second_sin, second_cos], axis=1),
        ],
        axis=0,
    )
    return (first_both, twist_cos, twist_sin, forward_second, inverse_second)


def spectrum(series, tables):
    first_both, twist_cos, twist_sin, forward_second, inverse_second = tables
    channels, length = series.shape
    rows_k = twist_cos.shape[0]
    half = first_both.shape[1]
    second_len = twist_cos.shape[1]
    blocks = series.reshape(channels, half, length // half)
    part = jnp.einsum("ka,cab->ckb", first_both, blocks, precision=HIGHEST)
    part_re = part[:, :rows_k]
    part_im = part[:, rows_k:]
    turn_re = part_re * twist_cos + part_im * twist_sin
    turn_im = part_im * twist_cos - part_re * twist_sin
    turned = jnp.concatenate([turn_re, turn_im], axis=2)
    result = jnp.einsum("ckb,bm->ckm", turned, forward_second, precision=HIGHEST)
    return (result[:, :, :second_len], result[:, :, second_len:])


def signal_of(pair, tables):
    first_both, twist_cos, twist_sin, forward_second, inverse_second = tables
    spec_re, spec_im = pair
    channels = spec_re.shape[0]
    second_len = twist_cos.shape[1]
    total = twist_cos.shape[0] * second_len
    joined = jnp.concatenate([spec_re, spec_im], axis=2)
    back = jnp.einsum("ckm,mb->ckb", joined, inverse_second, precision=HIGHEST)
    back_re = back[:, :, :second_len]
    back_im = back[:, :, second_len:]
    turn_re = back_re * twist_cos - back_im * twist_sin
    turn_im = back_im * twist_cos + back_re * twist_sin
    turned = jnp.concatenate([turn_re, turn_im], axis=1)
    blocks = jnp.einsum("ka,ckb->cab", first_both, turned, precision=HIGHEST)
    return blocks.reshape(channels, -1) * (1.0 / total)


def product(left, right, conjugate):
    left_re, left_im = left
    right_re, right_im = right
    if conjugate:
        right_im = -right_im
    return (left_re * right_re - left_im * right_im, left_re * right_im + left_im * right_re)


def widen(array):
    return array.astype(jnp.float32)


def local(token_ids, field_offsets, embed_table, w_in, short_taps, filters, cotangent):
    tok_rows, width = cotangent.shape
    peers = lax.axis_size("tm")
    fields = token_ids.shape[1]
    codes = embed_table.shape[0] // fields
    rows = w_in.shape[0]
    chans = width // peers
    steps = tok_rows * peers

    ids = lax.all_to_all(
        jnp.broadcast_to(token_ids.T.astype(jnp.bfloat16)[None], (peers, fields, tok_rows)),
        "tm",
        split_axis=0,
        concat_axis=0,
        tiled=True,
    )
    ids = ids.transpose(1, 0, 2).reshape(fields, steps)
    w_moved = lax.all_to_all(
        w_in.reshape(rows, 3, peers, chans).transpose(2, 0, 1, 3),
        "tm",
        split_axis=0,
        concat_axis=0,
        tiled=True,
    )
    w_cols = w_moved.reshape(width, 3 * chans)
    cot_moved = lax.all_to_all(
        cotangent.T.reshape(peers, chans, tok_rows), "tm", split_axis=0, concat_axis=0, tiled=True
    )
    upstream = widen(cot_moved.transpose(1, 0, 2).reshape(chans, steps))

    entries = jnp.concatenate(
        [
            lax.dynamic_slice_in_dim(embed_table, field_offsets[f], codes, axis=0)
            for f in range(fields)
        ],
        axis=0,
    )
    hot = (
        jnp.arange(codes, dtype=jnp.int32)[None, :, None] == ids.astype(jnp.int32)[:, None, :]
    ).astype(jnp.bfloat16)
    hot = hot.reshape(fields * codes, steps)
    coded = jnp.dot(entries, w_cols, preferred_element_type=jnp.float32).astype(jnp.bfloat16)
    proj = jnp.einsum("ec,et->ct", coded, hot, preferred_element_type=jnp.float32)
    proj = widen(proj.astype(jnp.bfloat16))
    taps = short_taps.reshape(3, 3, peers, chans)
    taps = lax.dynamic_index_in_dim(taps, lax.axis_index("tm"), axis=2, keepdims=False)
    taps = taps.reshape(3, 3 * chans, 1)
    late1 = jnp.pad(proj, ((0, 0), (1, 0)))[:, :steps]
    late2 = jnp.pad(proj, ((0, 0), (2, 0)))[:, :steps]
    mixed = (taps[0] * proj + taps[1] * late1 + taps[2] * late2).astype(jnp.bfloat16)
    values = widen(mixed[:chans])
    first_gate = widen(mixed[chans : 2 * chans])
    second_gate = widen(mixed[2 * chans :])

    total = 2 * steps
    bits = total.bit_length() - 1
    first_len = 1 << (bits + 1) // 2
    second_len = total // first_len
    tables = build_tables(first_len, second_len, total)
    first_spec = spectrum(widen(filters[0]), tables)
    second_spec = spectrum(widen(filters[1]), tables)

    def rounded(value):
        return widen(value.astype(jnp.bfloat16))

    value_spec = spectrum(values, tables)
    first_conv = rounded(signal_of(product(value_spec, first_spec, False), tables))
    first_mix = rounded(first_gate * first_conv)
    mix_spec = spectrum(first_mix, tables)
    second_conv = rounded(signal_of(product(mix_spec, second_spec, False), tables))
    mixer_out = (second_gate * second_conv).astype(jnp.bfloat16)
    mixer_moved = lax.all_to_all(
        mixer_out.reshape(chans, peers, tok_rows).transpose(1, 0, 2),
        "tm",
        split_axis=0,
        concat_axis=0,
        tiled=True,
    )
    mixer_out = mixer_moved.reshape(width, tok_rows).T
    grad_conv2 = rounded(upstream * second_gate)
    grad_gate2 = rounded(upstream * second_conv)
    grad_spec2 = spectrum(grad_conv2, tables)
    grad_mix = rounded(signal_of(product(grad_spec2, second_spec, True), tables))
    filter_two = signal_of(product(grad_spec2, mix_spec, True), tables)
    grad_gate1 = rounded(grad_mix * first_conv)
    grad_conv1 = rounded(grad_mix * first_gate)
    grad_spec1 = spectrum(grad_conv1, tables)
    grad_values = rounded(signal_of(product(grad_spec1, first_spec, True), tables))
    filter_one = signal_of(product(grad_spec1, value_spec, True), tables)
    filter_grads = jnp.stack([filter_one, filter_two], axis=0)
    grad_mixed = jnp.concatenate([grad_values, grad_gate1, grad_gate2], axis=0)
    soon1 = jnp.pad(grad_mixed, ((0, 0), (0, 1)))[:, 1:]
    soon2 = jnp.pad(grad_mixed, ((0, 0), (0, 2)))[:, 2:]
    grad_proj = (taps[0] * grad_mixed + taps[1] * soon1 + taps[2] * soon2).astype(jnp.bfloat16)
    tap_terms = jnp.stack(
        [jnp.sum(grad_mixed * moved, axis=1) for moved in (proj, late1, late2)], axis=0
    )
    coded_grads = jnp.einsum("ct,et->ce", grad_proj, hot, preferred_element_type=jnp.float32)
    weight_part = jnp.einsum(
        "er,ce->rc", entries, coded_grads.astype(jnp.bfloat16), preferred_element_type=jnp.float32
    )
    weight_moved = lax.all_to_all(
        weight_part.astype(jnp.bfloat16).reshape(peers, rows, 3 * chans),
        "tm",
        split_axis=0,
        concat_axis=0,
        tiled=True,
    )
    weight_grads = widen(weight_moved).reshape(peers, rows, 3, chans).transpose(1, 2, 0, 3)
    tap_moved = lax.all_to_all(
        jnp.broadcast_to(tap_terms[None], (peers, 3, 3 * chans)),
        "tm",
        split_axis=0,
        concat_axis=0,
        tiled=True,
    )
    tap_grads = tap_moved.reshape(peers, 3, 3, chans).transpose(1, 2, 0, 3)
    return (
        mixer_out,
        weight_grads.reshape(rows, 3 * width),
        tap_grads.reshape(3, 3 * width),
        filter_grads,
    )


def solution(mesh):
    return jax.shard_map(
        local,
        mesh=mesh,
        in_specs=(
            P(("groups", "tm"), None),
            P("groups"),
            P(),
            P("tm", None),
            P(),
            P(None, "tm", None),
            P(("groups", "tm"), None),
        ),
        out_specs=(
            P(("groups", "tm"), None),
            P(("groups", "tm"), None),
            P("groups", None),
            P("groups", "tm", None),
        ),
        check_vma=False,
    )
```

```python
import jax
import jax.numpy as jnp
import ml_dtypes
import numpy as np
from jax import lax
from jax.experimental import pallas as pl
from jax.experimental.pallas import tpu as pltpu
from jax.sharding import PartitionSpec as P

F32 = jnp.float32
BF16 = jnp.bfloat16
LANES = 128
GROUP = 16
PARAMS = pltpu.CompilerParams(vmem_limit_bytes=48 * 1024 * 1024)


def widen(array):
    return array.astype(F32)


def rounded(array):
    return array.astype(BF16).astype(F32)


def transform_tables(blocks):
    total = 2 * blocks * LANES
    row = np.arange(blocks) + 0.5
    first = np.exp(-2j * np.pi * np.outer(row, np.arange(blocks)) / (2 * blocks))
    turn = np.exp(-2j * np.pi * np.outer(row, np.arange(LANES)) / total)
    second = np.exp(-2j * np.pi * np.outer(np.arange(LANES), np.arange(LANES)) / LANES)
    same = np.eye(GROUP)
    first_rows = np.concatenate([first.real, first.imag], axis=0)
    back_rows = np.concatenate([first.real.T, first.imag.T], axis=1) * (2.0 / total)
    forward = np.block([[second.real, second.imag], [-second.imag, second.real]])
    inverse = np.block([[second.real, -second.imag], [second.imag, second.real]])
    narrow = ml_dtypes.bfloat16
    return (
        np.kron(first_rows, same).astype(narrow),
        np.kron(back_rows, same).astype(narrow),
        forward.astype(narrow),
        inverse.astype(narrow),
        np.repeat(turn.real, GROUP, axis=0).astype(np.float32),
        np.repeat(turn.imag, GROUP, axis=0).astype(np.float32),
    )


def dot(left, right):
    return jnp.dot(left, right, preferred_element_type=F32)


def joined(parts, axis):
    return parts[0] if len(parts) == 1 else jnp.concatenate(parts, axis=axis)


def forward(series, tables):
    first, _, second, _, turn_re, turn_im = tables
    rows = turn_re.shape[0]
    part = dot(first[...], joined(series, 1))
    spectra = []
    for place in range(len(series)):
        lanes = slice(place * LANES, (place + 1) * LANES)
        part_re = part[:rows, lanes]
        part_im = part[rows:, lanes]
        turned = jnp.concatenate(
            [
                part_re * turn_re[...] - part_im * turn_im[...],
                part_re * turn_im[...] + part_im * turn_re[...],
            ],
            axis=1,
        )
        spectra.append(dot(turned.astype(BF16), second[...]))
    return spectra


def inverse(spectra, tables):
    _, last, _, second, turn_re, turn_im = tables
    turned = []
    for spectrum in spectra:
        back = dot(spectrum.astype(BF16), second[...])
        back_re = back[:, :LANES]
        back_im = back[:, LANES:]
        turned.append(
            jnp.concatenate(
                [
                    back_re * turn_re[...] + back_im * turn_im[...],
                    back_im * turn_re[...] - back_re * turn_im[...],
                ],
                axis=0,
            ).astype(BF16)
        )
    signal = dot(last[...], joined(turned, 1))
    return [signal[:, place * LANES : (place + 1) * LANES] for place in range(len(spectra))]


def product(left, right, conjugate):
    left_re, left_im = left[:, :LANES], left[:, LANES:]
    right_re, right_im = right[:, :LANES], right[:, LANES:]
    if conjugate:
        return jnp.concatenate(
            [
                left_re * right_re + left_im * right_im,
                left_im * right_re - left_re * right_im,
            ],
            axis=1,
        )
    return jnp.concatenate(
        [
            left_re * right_re - left_im * right_im,
            left_re * right_im + left_im * right_re,
        ],
        axis=1,
    )


def batches(chans):
    groups = chans // GROUP
    size = 2 if groups % 2 == 0 else 1
    return [range(start, start + size) for start in range(0, groups, size)]


def channel_rows(group, offset=0):
    return slice(offset + group * GROUP, offset + (group + 1) * GROUP)


def flat(block):
    return block.reshape(block.shape[0] * block.shape[1], block.shape[2])


def one_hot(ids, codes):
    fields, lanes = ids.shape
    code = lax.broadcasted_iota(jnp.int32, (codes, lanes), 0).astype(F32)
    return jnp.concatenate(
        [
            jnp.where(code == ids[field : field + 1], 1.0, 0.0).astype(BF16)
            for field in range(fields)
        ],
        axis=0,
    )


def filter_kernel(filters, *rest):
    tables, spectra = rest[:6], rest[6]
    chans, steps = filters.shape[1:]
    blocks = steps // LANES
    for which in range(2):
        for batch in batches(chans):
            series = [
                jnp.concatenate(
                    [
                        filters[which, channel_rows(group), t * LANES : (t + 1) * LANES]
                        for t in range(blocks)
                    ],
                    axis=0,
                )
                for group in batch
            ]
            for group, spectrum in zip(batch, forward(series, tables)):
                spectra[which, group] = spectrum


def forward_kernel(ids, entries, w_cols, taps, filter_spec, *rest):
    tables = rest[:6]
    proj, mixed, first_conv, second_conv, value_spec, mix_spec, mixer_out = rest[6:]
    blocks, fields, _ = ids.shape
    codes = entries.shape[0] // fields
    chans = w_cols.shape[1] // 3
    coded = dot(entries[...], w_cols[...]).T.astype(BF16)
    lane = lax.broadcasted_iota(jnp.int32, (3 * chans, LANES), 1)
    last1 = jnp.zeros((3 * chans, LANES), F32)
    last2 = last1
    for pair in range(blocks // 2):
        hot = jnp.concatenate(
            [one_hot(widen(ids[2 * pair + side]), codes) for side in range(2)], axis=1
        )
        both = dot(coded, hot).astype(BF16)
        for side in range(2):
            block = 2 * pair + side
            now = both[:, side * LANES : (side + 1) * LANES]
            proj[block] = now
            now = widen(now)
            turn1 = pltpu.roll(now, 1, 1)
            turn2 = pltpu.roll(now, 2, 1)
            late1 = jnp.where(lane < 1, last1, turn1)
            late2 = jnp.where(lane < 2, last2, turn2)
            last1, last2 = turn1, turn2
            mixed[block] = (taps[0] * now + taps[1] * late1 + taps[2] * late2).astype(BF16)
    for batch in batches(chans):
        spectra = forward([flat(mixed[:, channel_rows(group), :]) for group in batch], tables)
        turned = []
        for group, spectrum in zip(batch, spectra):
            value_spec[group] = spectrum
            turned.append(product(spectrum, filter_spec[0, group], False))
        series = []
        for group, signal in zip(batch, inverse(turned, tables)):
            conv = signal.astype(BF16)
            first_conv[:, channel_rows(group), :] = conv.reshape(blocks, GROUP, LANES)
            gate = flat(mixed[:, channel_rows(group, chans), :])
            series.append((widen(gate) * widen(conv)).astype(BF16))
        turned = []
        for group, spectrum in zip(batch, forward(series, tables)):
            mix_spec[group] = spectrum
            turned.append(product(spectrum, filter_spec[1, group], False))
        for group, signal in zip(batch, inverse(turned, tables)):
            conv = signal.astype(BF16)
            second_conv[:, channel_rows(group), :] = conv.reshape(blocks, GROUP, LANES)
            gate = flat(mixed[:, channel_rows(group, 2 * chans), :])
            result = (widen(gate) * widen(conv)).astype(BF16)
            mixer_out[:, channel_rows(group), :] = result.reshape(blocks, GROUP, LANES)


def backward_kernel(
    ids, entries, taps, filter_spec, cotangent, proj, mixed, first_conv, second_conv, *rest
):
    tables = rest[:6]
    weight_part, tap_terms, grad_spec, grad_mixed, grad_proj, hot = rest[6:]
    blocks, fields, _ = ids.shape
    codes = entries.shape[0] // fields
    chans = cotangent.shape[1]
    for batch in batches(chans):
        series = []
        for group in batch:
            upstream = widen(flat(cotangent[:, channel_rows(group), :]))
            gate = widen(flat(mixed[:, channel_rows(group, 2 * chans), :]))
            conv = widen(flat(second_conv[:, channel_rows(group), :]))
            series.append((upstream * gate).astype(BF16))
            grad_mixed[:, channel_rows(group, 2 * chans), :] = (
                (upstream * conv).astype(BF16).reshape(blocks, GROUP, LANES)
            )
        turned = []
        for group, spectrum in zip(batch, forward(series, tables)):
            grad_spec[1, group] = spectrum
            turned.append(product(spectrum, filter_spec[1, group], True))
        series = []
        for group, signal in zip(batch, inverse(turned, tables)):
            grad_mix = rounded(signal)
            gate = widen(flat(mixed[:, channel_rows(group, chans), :]))
            conv = widen(flat(first_conv[:, channel_rows(group), :]))
            series.append((grad_mix * gate).astype(BF16))
            grad_mixed[:, channel_rows(group, chans), :] = (
                (grad_mix * conv).astype(BF16).reshape(blocks, GROUP, LANES)
            )
        turned = []
        for group, spectrum in zip(batch, forward(series, tables)):
            grad_spec[0, group] = spectrum
            turned.append(product(spectrum, filter_spec[0, group], True))
        for group, signal in zip(batch, inverse(turned, tables)):
            grad_mixed[:, channel_rows(group), :] = signal.astype(BF16).reshape(
                blocks, GROUP, LANES
            )
    lane = lax.broadcasted_iota(jnp.int32, (3 * chans, LANES), 1)
    next1 = jnp.zeros((3 * chans, LANES), F32)
    next2 = next1
    sums = [next1] * 3
    for block in reversed(range(blocks)):
        lanes = slice(block * LANES, (block + 1) * LANES)
        hot[:, lanes] = one_hot(widen(ids[block]), codes)
        now = widen(grad_mixed[block])
        turn1 = pltpu.roll(now, LANES - 1, 1)
        turn2 = pltpu.roll(now, LANES - 2, 1)
        soon1 = jnp.where(lane >= LANES - 1, next1, turn1)
        soon2 = jnp.where(lane >= LANES - 2, next2, turn2)
        next1, next2 = turn1, turn2
        grad_proj[:, lanes] = (taps[0] * now + taps[1] * soon1 + taps[2] * soon2).astype(BF16)
        held = widen(proj[block])
        sums = [total + held * moved for total, moved in zip(sums, (now, soon1, soon2))]
    for tap in range(3):
        tap_terms[tap] = jnp.sum(sums[tap], axis=1, keepdims=True)
    coded = lax.dot_general(
        grad_proj[...], hot[...], (((1,), (1,)), ((), ())), preferred_element_type=F32
    )
    weight_part[...] = dot(coded.astype(BF16), entries[...]).T.astype(BF16)


def lagged_kernel(grad_spec, value_spec, mix_spec, *rest):
    tables, filter_grads = rest[:6], rest[6]
    chans, steps = filter_grads.shape[1:]
    blocks = steps // LANES
    for which, other in enumerate((value_spec, mix_spec)):
        for batch in batches(chans):
            turned = [product(grad_spec[which, group], other[group], True) for group in batch]
            for group, signal in zip(batch, inverse(turned, tables)):
                for t in range(blocks):
                    filter_grads[which, channel_rows(group), t * LANES : (t + 1) * LANES] = signal[
                        t * GROUP : (t + 1) * GROUP
                    ]


def shape(dims, kind):
    return jax.ShapeDtypeStruct(dims, kind)


def exchange(blocks):
    return lax.all_to_all(blocks, "tm", split_axis=0, concat_axis=0, tiled=True)


def local(token_ids, field_offsets, embed_table, w_in, short_taps, filters, cotangent):
    tok_rows, width = cotangent.shape
    peers = lax.axis_size("tm")
    fields = token_ids.shape[1]
    codes = embed_table.shape[0] // fields
    rows = w_in.shape[0]
    chans = width // peers
    steps = tok_rows * peers
    groups = chans // GROUP
    tables = transform_tables(peers)

    w_send = w_in.reshape(rows, 3, peers, chans).transpose(2, 0, 1, 3)
    w_send = w_send.reshape(peers, rows * 3 * chans // LANES, LANES)
    ids_send = jnp.broadcast_to(token_ids.T.astype(BF16)[None], (peers, fields, tok_rows))
    arrived = exchange(jnp.concatenate([w_send, ids_send], axis=1))
    w_cols = arrived[:, : w_send.shape[1]].reshape(width, 3 * chans)
    ids = arrived[:, w_send.shape[1] :]
    upstream = exchange(cotangent.T.reshape(peers, chans, tok_rows))

    entries = jnp.concatenate(
        [
            lax.dynamic_slice_in_dim(embed_table, field_offsets[f], codes, axis=0)
            for f in range(fields)
        ],
        axis=0,
    )
    taps = short_taps.reshape(3, 3, peers, chans)
    taps = lax.dynamic_index_in_dim(taps, lax.axis_index("tm"), axis=2, keepdims=False)
    taps = jnp.broadcast_to(taps.reshape(3, 3 * chans, 1), (3, 3 * chans, LANES))

    spec = (groups, peers * GROUP, 2 * LANES)
    moved = (peers, chans, LANES)
    wide = (peers, 3 * chans, LANES)
    filter_spec = pl.pallas_call(
        filter_kernel, out_shape=shape((2,) + spec, F32), compiler_params=PARAMS
    )(filters, *tables)
    proj, mixed, first_conv, second_conv, value_spec, mix_spec, mixer_out = pl.pallas_call(
        forward_kernel,
        out_shape=(
            shape(wide, BF16),
            shape(wide, BF16),
            shape(moved, BF16),
            shape(moved, BF16),
            shape(spec, F32),
            shape(spec, F32),
            shape(moved, BF16),
        ),
        compiler_params=PARAMS,
    )(ids, entries, w_cols, taps, filter_spec, *tables)
    mixer_out = exchange(mixer_out).reshape(width, tok_rows).T
    weight_part, tap_terms, grad_spec = pl.pallas_call(
        backward_kernel,
        out_shape=(
            shape((width, 3 * chans), BF16),
            shape((3, 3 * chans, 1), F32),
            shape((2,) + spec, F32),
        ),
        scratch_shapes=[
            pltpu.VMEM(wide, BF16),
            pltpu.VMEM((3 * chans, steps), BF16),
            pltpu.VMEM((fields * codes, steps), BF16),
        ],
        compiler_params=PARAMS,
    )(ids, entries, taps, filter_spec, upstream, proj, mixed, first_conv, second_conv, *tables)
    filter_grads = pl.pallas_call(
        lagged_kernel, out_shape=shape((2, chans, steps), F32), compiler_params=PARAMS
    )(grad_spec, value_spec, mix_spec, *tables)

    tap_terms = tap_terms.reshape(1, 3 * 3 * chans)
    tap_high = tap_terms.astype(BF16)
    tap_low = (tap_terms - widen(tap_high)).astype(BF16)
    tap_send = jnp.concatenate([tap_high, tap_low], axis=1)
    space = -tap_send.shape[1] % LANES
    tap_send = jnp.pad(tap_send, ((0, 0), (0, space))).reshape(1, -1, LANES)
    tap_send = jnp.broadcast_to(tap_send, (peers,) + tap_send.shape[1:])
    weight_send = weight_part.reshape(peers, rows * 3 * chans // LANES, LANES)
    arrived = exchange(jnp.concatenate([weight_send, tap_send], axis=1))
    weight_grads = arrived[:, : weight_send.shape[1]].reshape(peers, rows, 3, chans)
    weight_grads = widen(weight_grads).transpose(1, 2, 0, 3).reshape(rows, 3 * width)
    taps_moved = arrived[:, weight_send.shape[1] :].reshape(peers, -1)
    count = 3 * 3 * chans
    tap_grads = widen(taps_moved[:, :count]) + widen(taps_moved[:, count : 2 * count])
    tap_grads = tap_grads.reshape(peers, 3, 3, chans).transpose(1, 2, 0, 3)
    return (mixer_out, weight_grads, tap_grads.reshape(3, 3 * width), filter_grads)


def solution(mesh):
    return jax.shard_map(
        local,
        mesh=mesh,
        in_specs=(
            P(("groups", "tm"), None),
            P("groups"),
            P(),
            P("tm", None),
            P(),
            P(None, "tm", None),
            P(("groups", "tm"), None),
        ),
        out_specs=(
            P(("groups", "tm"), None),
            P(("groups", "tm"), None),
            P("groups", None),
            P("groups", "tm", None),
        ),
        check_vma=False,
    )
```

```python
import functools


import jax
import jax.numpy as jnp
import ml_dtypes
import numpy as np
from jax import lax
from jax.experimental import pallas as pl
from jax.experimental.pallas import tpu as pltpu
from jax.sharding import PartitionSpec as P

F32 = jnp.float32
BF16 = jnp.bfloat16
LANES = 128
GROUP = 16


def widen(array):
    return array.astype(F32)


def rounded(array):
    return array.astype(BF16).astype(F32)


def transform_tables(blocks):
    total = 2 * blocks * LANES
    row = np.arange(blocks) + 0.5
    first = np.exp(-2j * np.pi * np.outer(row, np.arange(blocks)) / (2 * blocks))
    turn = np.exp(-2j * np.pi * np.outer(row, np.arange(LANES)) / total)
    second = np.exp(-2j * np.pi * np.outer(np.arange(LANES), np.arange(LANES)) / LANES)
    same = np.eye(GROUP)
    first_rows = np.concatenate([first.real, first.imag], axis=0)
    back_rows = np.concatenate([first.real.T, first.imag.T], axis=1) * (2.0 / total)
    forward = np.block([[second.real, second.imag], [-second.imag, second.real]])
    inverse = np.block([[second.real, -second.imag], [second.imag, second.real]])
    narrow = ml_dtypes.bfloat16
    return (
        np.kron(first_rows, same).astype(narrow),
        np.kron(back_rows, same).astype(narrow),
        forward.astype(narrow),
        inverse.astype(narrow),
        np.repeat(turn.real, GROUP, axis=0).astype(np.float32),
        np.repeat(turn.imag, GROUP, axis=0).astype(np.float32),
    )


def dot(left, right):
    return jnp.dot(left, right, preferred_element_type=F32)


def joined(parts, axis):
    return parts[0] if len(parts) == 1 else jnp.concatenate(parts, axis=axis)


def forward(series, tables):
    first, _, second, _, turn_re, turn_im = tables
    rows = turn_re.shape[0]
    part = dot(first[...], joined(series, 1))
    spectra = []
    for place in range(len(series)):
        lanes = slice(place * LANES, (place + 1) * LANES)
        part_re = part[:rows, lanes]
        part_im = part[rows:, lanes]
        turned = jnp.concatenate(
            [
                part_re * turn_re[...] - part_im * turn_im[...],
                part_re * turn_im[...] + part_im * turn_re[...],
            ],
            axis=1,
        )
        spectra.append(dot(turned.astype(BF16), second[...]))
    return spectra


def inverse(spectra, tables):
    _, last, _, second, turn_re, turn_im = tables
    turned = []
    for spectrum in spectra:
        back = dot(spectrum.astype(BF16), second[...])
        back_re = back[:, :LANES]
        back_im = back[:, LANES:]
        turned.append(
            jnp.concatenate(
                [
                    back_re * turn_re[...] + back_im * turn_im[...],
                    back_im * turn_re[...] - back_re * turn_im[...],
                ],
                axis=0,
            ).astype(BF16)
        )
    signal = dot(last[...], joined(turned, 1))
    return [signal[:, place * LANES : (place + 1) * LANES] for place in range(len(spectra))]


def product(left, right, conjugate):
    left_re, left_im = left[:, :LANES], left[:, LANES:]
    right_re, right_im = right[:, :LANES], right[:, LANES:]
    if conjugate:
        return jnp.concatenate(
            [
                left_re * right_re + left_im * right_im,
                left_im * right_re - left_re * right_im,
            ],
            axis=1,
        )
    return jnp.concatenate(
        [
            left_re * right_re - left_im * right_im,
            left_re * right_im + left_im * right_re,
        ],
        axis=1,
    )


def batches(chans):
    groups = chans // GROUP
    size = 2 if groups % 2 == 0 else 1
    return [range(start, start + size) for start in range(0, groups, size)]


def channel_rows(group, offset=0):
    return slice(offset + group * GROUP, offset + (group + 1) * GROUP)


def flat(block):
    return block.reshape(block.shape[0] * block.shape[1], block.shape[2])


def one_hot(ids, codes):
    fields, lanes = ids.shape
    code = lax.broadcasted_iota(jnp.int32, (codes, lanes), 0).astype(F32)
    return jnp.concatenate(
        [
            jnp.where(code == ids[field : field + 1], 1.0, 0.0).astype(BF16)
            for field in range(fields)
        ],
        axis=0,
    )


def prepare_kernel(offsets, filters, table, *rest):
    tables = rest[:6]
    spectra, entries = rest[6:]
    chans, steps = filters.shape[1:]
    blocks = steps // LANES
    fields = offsets.shape[0]
    codes = entries.shape[0] // fields
    window = codes + GROUP
    for field in range(fields):
        start = jnp.minimum(offsets[field] // GROUP * GROUP, table.shape[0] - window)
        row = lax.broadcasted_iota(jnp.int32, (codes, window), 0) + (offsets[field] - start)
        place = lax.broadcasted_iota(jnp.int32, (codes, window), 1)
        picked = jnp.where(row == place, 1.0, 0.0).astype(BF16)
        entries[field * codes : (field + 1) * codes, :] = dot(
            picked, table[pl.ds(pl.multiple_of(start, GROUP), window), :]
        ).astype(BF16)
    for which in range(2):
        for batch in batches(chans):
            series = [
                jnp.concatenate(
                    [
                        filters[which, channel_rows(group), t * LANES : (t + 1) * LANES]
                        for t in range(blocks)
                    ],
                    axis=0,
                )
                for group in batch
            ]
            for group, spectrum in zip(batch, forward(series, tables)):
                spectra[which, group] = spectrum


def halves(array):
    lane = lax.broadcasted_iota(jnp.int32, array.shape, 1)
    return pltpu.roll(array, LANES // 2, 1), lane < LANES // 2


def packed_parts(rows):
    half = rows // 2
    marks = [0, rows, rows + half, 2 * rows + half, 2 * rows + half + 16]
    return [slice(low, high) for low, high in zip(marks[:-1], marks[1:])]


def pack_kernel(token_ids, w_in, cotangent, packed):
    peers = packed.shape[0]
    rows, wide = w_in.shape
    half = rows // 2
    part_two, part_one, part_time, part_ids = packed_parts(rows)
    fields = token_ids.shape[1]
    ids = jnp.concatenate(
        [widen(token_ids[...]), jnp.zeros((token_ids.shape[0], LANES - fields), F32)], axis=1
    )
    ids = ids.T[:16].astype(BF16)
    for pair in range(peers // 2):
        tiles = []
        for column in range(3):
            start = column * (wide // 3) + pair * LANES
            tile = widen(w_in[:, start : start + LANES])
            turned, first = halves(tile)
            tiles.append((tile, turned))
        first_half = first[:half]
        (zero, zero_turned), (one, one_turned), (two, two_turned) = tiles
        even, odd = 2 * pair, 2 * pair + 1
        packed[even, part_two, :] = jnp.where(first, zero, one_turned).astype(BF16)
        packed[odd, part_two, :] = jnp.where(first, zero_turned, one).astype(BF16)
        packed[even, part_one, :] = jnp.where(first_half, two[:half], two_turned[half:]).astype(
            BF16
        )
        packed[odd, part_one, :] = jnp.where(first_half, two_turned[:half], two[half:]).astype(
            BF16
        )
        turned = widen(cotangent[:, pair * LANES : (pair + 1) * LANES]).T.astype(BF16)
        packed[even, part_time, :] = turned[:rows]
        packed[odd, part_time, :] = turned[rows:]
        packed[even, part_ids, :] = ids
        packed[odd, part_ids, :] = ids


def unpack_kernel(packed, mixer_out, weight_grads, tap_grads):
    peers = packed.shape[0]
    rows, wide = weight_grads.shape
    half = rows // 2
    part_two, part_one, part_time, part_taps = packed_parts(rows)
    for pair in range(peers // 2):
        even, odd = 2 * pair, 2 * pair + 1
        starts = [column * (wide // 3) + pair * LANES for column in range(3)]
        lanes = [slice(start, start + LANES) for start in starts]

        def merged(low, high):
            low_turned, first = halves(low)
            high_turned, _ = halves(high)
            return jnp.where(first, low, high_turned), jnp.where(first, low_turned, high)

        zero, one = merged(widen(packed[even, part_two, :]), widen(packed[odd, part_two, :]))
        weight_grads[:, lanes[0]] = zero
        weight_grads[:, lanes[1]] = one
        upper, lower = merged(widen(packed[even, part_one, :]), widen(packed[odd, part_one, :]))
        weight_grads[:half, lanes[2]] = upper
        weight_grads[half:, lanes[2]] = lower
        both = widen(jnp.concatenate([packed[even, part_time, :], packed[odd, part_time, :]], 0))
        mixer_out[:, pair * LANES : (pair + 1) * LANES] = both.T.astype(BF16)
        low = widen(packed[even, part_taps, :])
        high = widen(packed[odd, part_taps, :])
        low = low[:8] + low[8:]
        high = high[:8] + high[8:]
        zero, one = merged(low, high)
        tap_grads[:, lanes[0]] = zero[:3]
        tap_grads[:, lanes[1]] = one[:3]
        tap_grads[:, lanes[2]] = zero[3:6]


def mixer_kernel(packed_form, *refs):
    if packed_form:
        arrived, refs = refs[0], refs[1:]
        chans = refs[0].shape[0] // arrived.shape[0]
        part_two, part_one, part_time, part_small = packed_parts(chans)
        width = refs[0].shape[1]
        fields = refs[0].shape[0] // LANES
        two = widen(flat(arrived[:, part_two, :]))
        one = widen(arrived[:, part_one, :])
        one_turned = pltpu.roll(flat(one), LANES // 2, 1).reshape(one.shape)
        one = flat(jnp.concatenate([one, one_turned], axis=1))
        w_cols = jnp.concatenate([two, one], axis=1).astype(BF16)
        cotangent = arrived.at[:, part_time, :]

        def ids_of(block):
            return widen(arrived[block, part_small, :])[:fields]

    else:
        w_cols, ids, cotangent = refs[0][...], refs[1], refs[2]
        refs = refs[3:]
        chans = cotangent.shape[1]

        def ids_of(block):
            return widen(ids[block])

    entries, taps, filter_spec = refs[:3]
    tables, refs = refs[3:9], refs[9:]
    if packed_form:
        sent, lagged_spec = refs[:2]
        refs = refs[2:]
        mixer_out = sent.at[:, part_time, :]
    else:
        mixer_out, weight_part, tap_terms, lagged_spec = refs[:4]
        refs = refs[4:]
    hot, proj, mixed, grad_mixed, grad_proj = refs
    blocks = mixed.shape[0]
    codes = LANES

    coded = dot(entries[...], w_cols).T[: 3 * chans].astype(BF16)
    lane = lax.broadcasted_iota(jnp.int32, (3 * chans, LANES), 1)
    last1 = jnp.zeros((3 * chans, LANES), F32)
    last2 = last1
    for pair in range(blocks // 2):
        lanes = slice(2 * pair * LANES, (2 * pair + 2) * LANES)
        hot[:, lanes] = jnp.concatenate(
            [one_hot(ids_of(2 * pair + side), codes) for side in range(2)], axis=1
        )
        both = dot(coded, hot[:, lanes]).astype(BF16)
        for side in range(2):
            block = 2 * pair + side
            now = both[:, side * LANES : (side + 1) * LANES]
            proj[block] = now
            now = widen(now)
            turn1 = pltpu.roll(now, 1, 1)
            turn2 = pltpu.roll(now, 2, 1)
            late1 = jnp.where(lane < 1, last1, turn1)
            late2 = jnp.where(lane < 2, last2, turn2)
            last1, last2 = turn1, turn2
            mixed[block] = (taps[0] * now + taps[1] * late1 + taps[2] * late2).astype(BF16)

    def column(ref, group, place=0):
        return flat(ref[:, channel_rows(group, place * chans), :])

    def blocked(value):
        return value.reshape(blocks, GROUP, LANES)

    for batch in batches(chans):
        value_spec = forward([column(mixed, group) for group in batch], tables)
        turned = [
            product(spectrum, filter_spec[0, group], False)
            for group, spectrum in zip(batch, value_spec)
        ]
        first_conv = [rounded(signal) for signal in inverse(turned, tables)]
        series = [
            (widen(column(mixed, group, 1)) * conv).astype(BF16)
            for group, conv in zip(batch, first_conv)
        ]
        mix_spec = forward(series, tables)
        turned = [
            product(spectrum, filter_spec[1, group], False)
            for group, spectrum in zip(batch, mix_spec)
        ]
        series = []
        for group, signal in zip(batch, inverse(turned, tables)):
            second_conv = rounded(signal)
            gate = widen(column(mixed, group, 2))
            upstream = widen(column(cotangent, group))
            mixer_out[:, channel_rows(group), :] = blocked((gate * second_conv).astype(BF16))
            grad_mixed[:, channel_rows(group, 2 * chans), :] = blocked(
                (upstream * second_conv).astype(BF16)
            )
            series.append((upstream * gate).astype(BF16))
        grad_spec = forward(series, tables)
        turned = []
        for place, group in enumerate(batch):
            lagged_spec[1, group] = product(grad_spec[place], mix_spec[place], True).astype(BF16)
            turned.append(product(grad_spec[place], filter_spec[1, group], True))
        series = []
        for place, signal in enumerate(inverse(turned, tables)):
            grad_mix = rounded(signal)
            group = batch[place]
            grad_mixed[:, channel_rows(group, chans), :] = blocked(
                (grad_mix * first_conv[place]).astype(BF16)
            )
            series.append((grad_mix * widen(column(mixed, group, 1))).astype(BF16))
        grad_spec = forward(series, tables)
        turned = []
        for place, group in enumerate(batch):
            lagged_spec[0, group] = product(grad_spec[place], value_spec[place], True).astype(BF16)
            turned.append(product(grad_spec[place], filter_spec[0, group], True))
        for group, signal in zip(batch, inverse(turned, tables)):
            grad_mixed[:, channel_rows(group), :] = blocked(signal.astype(BF16))

    next1 = jnp.zeros((3 * chans, LANES), F32)
    next2 = next1
    sums = [next1] * 3
    for block in reversed(range(blocks)):
        now = widen(grad_mixed[block])
        turn1 = pltpu.roll(now, LANES - 1, 1)
        turn2 = pltpu.roll(now, LANES - 2, 1)
        soon1 = jnp.where(lane >= LANES - 1, next1, turn1)
        soon2 = jnp.where(lane >= LANES - 2, next2, turn2)
        next1, next2 = turn1, turn2
        grad_proj[:, block * LANES : (block + 1) * LANES] = (
            taps[0] * now + taps[1] * soon1 + taps[2] * soon2
        ).astype(BF16)
        held = widen(proj[block])
        sums = [total + held * moved for total, moved in zip(sums, (now, soon1, soon2))]
    coded = lax.dot_general(
        grad_proj[...], hot[...], (((1,), (1,)), ((), ())), preferred_element_type=F32
    )
    weights = dot(coded.astype(BF16), entries[...])
    if not packed_form:
        weight_part[...] = weights.T.astype(BF16)
        for tap in range(3):
            tap_terms[tap] = jnp.sum(sums[tap], axis=1, keepdims=True)
        return
    for tap in range(3):
        sums[tap] = jnp.sum(sums[tap].T, axis=0, keepdims=True)
    space = jnp.zeros((1, LANES), F32)
    total = jnp.concatenate(
        [sums[tap][:, :LANES] for tap in range(3)]
        + [
            jnp.concatenate([sums[tap][:, LANES:], space[:, : LANES - chans]], axis=1)
            for tap in range(3)
        ]
        + [space] * 2,
        axis=0,
    )
    high = rounded(total)
    small = jnp.concatenate([high, total - high], axis=0).astype(BF16)
    two = weights[: 2 * chans].T
    one = jnp.concatenate([weights[2 * chans :], jnp.zeros((LANES - chans, width), F32)], axis=0).T
    one = one.reshape(blocks, chans, LANES)
    half = chans // 2
    turned = pltpu.roll(flat(one[:, half:]), LANES // 2, 1)
    one = flat(one[:, :half])
    one = jnp.where(lax.broadcasted_iota(jnp.int32, one.shape, 1) < LANES // 2, one, turned)
    sent[:, part_two, :] = two.astype(BF16).reshape(blocks, chans, LANES)
    sent[:, part_one, :] = one.astype(BF16).reshape(blocks, half, LANES)
    for block in range(blocks):
        sent[block, part_small, :] = small


def lagged_kernel(lagged_spec, *rest):
    tables, filter_grads = rest[:6], rest[6]
    chans, steps = filter_grads.shape[1:]
    blocks = steps // LANES
    for which in range(2):
        for batch in batches(chans):
            turned = [lagged_spec[which, group] for group in batch]
            for group, signal in zip(batch, inverse(turned, tables)):
                for t in range(blocks):
                    filter_grads[which, channel_rows(group), t * LANES : (t + 1) * LANES] = signal[
                        t * GROUP : (t + 1) * GROUP
                    ]


def shape(dims, kind):
    return jax.ShapeDtypeStruct(dims, kind)


def exchange(blocks):
    return lax.all_to_all(blocks, "tm", split_axis=0, concat_axis=0, tiled=True)


def call(kernel, name, megabytes, **settings):
    return pl.pallas_call(
        kernel,
        name=name,
        compiler_params=pltpu.CompilerParams(vmem_limit_bytes=megabytes * 1024 * 1024),
        **settings,
    )


def send_inputs(token_ids, w_in, cotangent, peers):
    tok_rows, width = cotangent.shape
    rows, fields, chans = w_in.shape[0], token_ids.shape[1], width // peers
    w_send = w_in.reshape(rows, 3, peers, chans).transpose(2, 0, 1, 3)
    w_send = w_send.reshape(peers, rows * 3 * chans // LANES, LANES)
    ids_send = jnp.broadcast_to(token_ids.T.astype(BF16)[None], (peers, fields, tok_rows))
    cot_send = cotangent.T.reshape(peers, chans, tok_rows)
    arrived = exchange(jnp.concatenate([w_send, ids_send, cot_send], axis=1))
    count = w_send.shape[1]
    w_cols = arrived[:, :count].reshape(width, 3 * chans)
    return w_cols, arrived[:, count : count + fields], arrived[:, count + fields :]


def send_results(mixer_out, weight_part, tap_terms, peers, rows):
    _, chans, tok_rows = mixer_out.shape
    width = peers * chans
    count = 9 * chans
    tap_terms = tap_terms.reshape(1, count)
    tap_high = tap_terms.astype(BF16)
    tap_low = (tap_terms - widen(tap_high)).astype(BF16)
    tap_send = jnp.concatenate([tap_high, tap_low], axis=1)
    tap_send = jnp.pad(tap_send, ((0, 0), (0, -2 * count % LANES))).reshape(1, -1, LANES)
    tap_send = jnp.broadcast_to(tap_send, (peers,) + tap_send.shape[1:])
    weight_send = weight_part.reshape(peers, rows * 3 * chans // LANES, LANES)
    arrived = exchange(jnp.concatenate([mixer_out, weight_send, tap_send], axis=1))
    mixer_out = arrived[:, :chans].reshape(width, tok_rows).T
    place = chans + weight_send.shape[1]
    weight_grads = arrived[:, chans:place].reshape(peers, rows, 3, chans)
    weight_grads = widen(weight_grads).transpose(1, 2, 0, 3).reshape(rows, 3 * width)
    taps_moved = arrived[:, place:].reshape(peers, -1)
    tap_grads = widen(taps_moved[:, :count]) + widen(taps_moved[:, count : 2 * count])
    tap_grads = tap_grads.reshape(peers, 3, 3, chans).transpose(1, 2, 0, 3)
    return mixer_out, weight_grads, tap_grads.reshape(3, 3 * width)


def local(token_ids, field_offsets, embed_table, w_in, short_taps, filters, cotangent):
    tok_rows, width = cotangent.shape
    peers = lax.axis_size("tm")
    fields = token_ids.shape[1]
    rows = w_in.shape[0]
    chans = width // peers
    steps = tok_rows * peers
    groups = chans // GROUP
    tables = transform_tables(peers)
    packed_form = 2 * chans == LANES and rows == chans and fields <= 8
    spec = (2, groups, peers * GROUP, 2 * LANES)
    moved = (peers, chans, LANES)
    wide = (peers, 3 * chans, LANES)
    packed = shape((peers, packed_parts(rows)[-1].stop, LANES), BF16)

    if packed_form:
        sent = call(pack_kernel, "pack", 16, out_shape=packed)(token_ids, w_in, cotangent)
        arrived = (exchange(sent),)
    else:
        arrived = send_inputs(token_ids, w_in, cotangent, peers)

    whole = pl.BlockSpec(memory_space=pltpu.VMEM)
    filter_spec, entries = call(
        prepare_kernel,
        "prepare",
        32,
        in_specs=[pl.BlockSpec(memory_space=pltpu.SMEM)] + [whole] * 8,
        out_shape=(shape(spec, F32), shape(embed_table.shape, BF16)),
        cost_estimate=pl.CostEstimate(
            flops=10**10, bytes_accessed=3 * 10**7, transcendentals=0
        ),
    )(field_offsets, filters, embed_table, *tables)
    taps = short_taps.reshape(3, 3, peers, chans)
    taps = lax.dynamic_index_in_dim(taps, lax.axis_index("tm"), axis=2, keepdims=False)
    taps = jnp.broadcast_to(taps.reshape(3, 3 * chans, 1), (3, 3 * chans, LANES))

    if packed_form:
        out_shape = (packed, shape(spec, BF16))
    else:
        out_shape = (
            shape(moved, BF16),
            shape((width, 3 * chans), BF16),
            shape((3, 3 * chans, 1), F32),
            shape(spec, BF16),
        )
    hot_bytes = 2 * embed_table.shape[0] * steps
    results = call(
        functools.partial(mixer_kernel, packed_form),
        "mixer",
        20 + 2 * hot_bytes // 2**20,
        out_shape=out_shape,
        scratch_shapes=[
            pltpu.VMEM((embed_table.shape[0], steps), BF16),
            pltpu.VMEM(wide, BF16),
            pltpu.VMEM(wide, BF16),
            pltpu.VMEM(wide, BF16),
            pltpu.VMEM((3 * chans, steps), BF16),
        ],
    )(*arrived, entries, taps, filter_spec, *tables)
    filter_grads = call(
        lagged_kernel,
        "lagged",
        24,
        out_shape=shape((2, chans, steps), F32),
        cost_estimate=pl.CostEstimate(
            flops=10**10, bytes_accessed=3 * 10**7, transcendentals=0
        ),
    )(results[-1], *tables)
    if packed_form:
        mixer_out, weight_grads, tap_grads = call(
            unpack_kernel,
            "unpack",
            16,
            out_shape=(
                shape((tok_rows, width), BF16),
                shape((rows, 3 * width), F32),
                shape((3, 3 * width), F32),
            ),
        )(exchange(results[0]))
    else:
        mixer_out, weight_grads, tap_grads = send_results(*results[:3], peers, rows)
    return (mixer_out, weight_grads, tap_grads, filter_grads)


def solution(mesh):
    return jax.shard_map(
        local,
        mesh=mesh,
        in_specs=(
            P(("groups", "tm"), None),
            P("groups"),
            P(),
            P("tm", None),
            P(),
            P(None, "tm", None),
            P(("groups", "tm"), None),
        ),
        out_specs=(
            P(("groups", "tm"), None),
            P(("groups", "tm"), None),
            P("groups", None),
            P("groups", "tm", None),
        ),
        check_vma=False,
    )
```

```python
import functools


import jax
import jax.numpy as jnp
import ml_dtypes
import numpy as np
from jax import lax
from jax.experimental import pallas as pl
from jax.experimental.pallas import tpu as pltpu
from jax.sharding import PartitionSpec as P

F32 = jnp.float32
BF16 = jnp.bfloat16
LANES = 128
GROUP = 16


def widen(array):
    return array.astype(F32)


def rounded(array):
    return array.astype(BF16).astype(F32)


def transform_tables(blocks):
    total = 2 * blocks * LANES
    row = np.arange(blocks) + 0.5
    first = np.exp(-2j * np.pi * np.outer(row, np.arange(blocks)) / (2 * blocks))
    turn = np.exp(-2j * np.pi * np.outer(row, np.arange(LANES)) / total)
    second = np.exp(-2j * np.pi * np.outer(np.arange(LANES), np.arange(LANES)) / LANES)
    same = np.eye(GROUP)
    first_rows = np.concatenate([first.real, first.imag], axis=0)
    back_rows = np.concatenate([first.real.T, first.imag.T], axis=1) * (2.0 / total)
    forward = np.block([[second.real, second.imag], [-second.imag, second.real]])
    inverse = np.block([[second.real, -second.imag], [second.imag, second.real]])
    narrow = ml_dtypes.bfloat16
    return (
        np.kron(first_rows, same).astype(narrow),
        np.kron(back_rows, same).astype(narrow),
        forward.astype(narrow),
        inverse.astype(narrow),
        np.repeat(turn.real, GROUP, axis=0).astype(np.float32),
        np.repeat(turn.imag, GROUP, axis=0).astype(np.float32),
    )


def dot(left, right):
    return jnp.dot(left, right, preferred_element_type=F32)


def joined(parts, axis):
    return parts[0] if len(parts) == 1 else jnp.concatenate(parts, axis=axis)


def forward(series, tables):
    first, _, second, _, turn_re, turn_im = tables
    rows = turn_re.shape[0]
    part = dot(first[...], joined(series, 1))
    spectra = []
    for place in range(len(series)):
        lanes = slice(place * LANES, (place + 1) * LANES)
        part_re = part[:rows, lanes]
        part_im = part[rows:, lanes]
        turned = jnp.concatenate(
            [
                part_re * turn_re[...] - part_im * turn_im[...],
                part_re * turn_im[...] + part_im * turn_re[...],
            ],
            axis=1,
        )
        spectra.append(dot(turned.astype(BF16), second[...]))
    return spectra


def inverse(spectra, tables):
    _, last, _, second, turn_re, turn_im = tables
    turned = []
    for spectrum in spectra:
        back = dot(spectrum.astype(BF16), second[...])
        back_re = back[:, :LANES]
        back_im = back[:, LANES:]
        turned.append(
            jnp.concatenate(
                [
                    back_re * turn_re[...] + back_im * turn_im[...],
                    back_im * turn_re[...] - back_re * turn_im[...],
                ],
                axis=0,
            ).astype(BF16)
        )
    signal = dot(last[...], joined(turned, 1))
    return [signal[:, place * LANES : (place + 1) * LANES] for place in range(len(spectra))]


def product(left, right, conjugate):
    left_re, left_im = left[:, :LANES], left[:, LANES:]
    right_re, right_im = right[:, :LANES], right[:, LANES:]
    if conjugate:
        return jnp.concatenate(
            [
                left_re * right_re + left_im * right_im,
                left_im * right_re - left_re * right_im,
            ],
            axis=1,
        )
    return jnp.concatenate(
        [
            left_re * right_re - left_im * right_im,
            left_re * right_im + left_im * right_re,
        ],
        axis=1,
    )


def batches(chans):
    groups = chans // GROUP
    size = 2 if groups % 2 == 0 else 1
    return [range(start, start + size) for start in range(0, groups, size)]


def channel_rows(group, offset=0):
    return slice(offset + group * GROUP, offset + (group + 1) * GROUP)


def flat(block):
    return block.reshape(block.shape[0] * block.shape[1], block.shape[2])


def one_hot(ids, codes):
    fields, lanes = ids.shape
    code = lax.broadcasted_iota(jnp.int32, (codes, lanes), 0).astype(F32)
    return jnp.concatenate(
        [
            jnp.where(code == ids[field : field + 1], 1.0, 0.0).astype(BF16)
            for field in range(fields)
        ],
        axis=0,
    )


def prepare_kernel(offsets, filters, table, *rest):
    tables = rest[:6]
    spectra, entries = rest[6:]
    chans, steps = filters.shape[1:]
    blocks = steps // LANES
    fields = offsets.shape[0]
    codes = entries.shape[0] // fields
    window = codes + GROUP
    for field in range(fields):
        start = jnp.minimum(offsets[field] // GROUP * GROUP, table.shape[0] - window)
        row = lax.broadcasted_iota(jnp.int32, (codes, window), 0) + (offsets[field] - start)
        place = lax.broadcasted_iota(jnp.int32, (codes, window), 1)
        picked = jnp.where(row == place, 1.0, 0.0).astype(BF16)
        entries[field * codes : (field + 1) * codes, :] = dot(
            picked, table[pl.ds(pl.multiple_of(start, GROUP), window), :]
        ).astype(BF16)
    for which in range(2):
        for batch in batches(chans):
            series = [
                jnp.concatenate(
                    [
                        filters[which, channel_rows(group), t * LANES : (t + 1) * LANES]
                        for t in range(blocks)
                    ],
                    axis=0,
                )
                for group in batch
            ]
            for group, spectrum in zip(batch, forward(series, tables)):
                spectra[which, group] = spectrum


def halves(array):
    lane = lax.broadcasted_iota(jnp.int32, array.shape, 1)
    return pltpu.roll(array, LANES // 2, 1), lane < LANES // 2


def packed_parts(rows):
    half = rows // 2
    marks = [0, rows, rows + half, 2 * rows + half, 2 * rows + half + 16]
    return [slice(low, high) for low, high in zip(marks[:-1], marks[1:])]


def pack_kernel(token_ids, w_in_far, cotangent_far, packed_far, w_in, cotangent, packed, sems):
    peers = packed.shape[0]
    rows, wide = w_in.shape
    half = rows // 2
    part_two, part_one, part_time, part_ids = packed_parts(rows)
    arrivals = [
        pltpu.make_async_copy(far, near, sems.at[place])
        for place, (far, near) in enumerate(((w_in_far, w_in), (cotangent_far, cotangent)))
    ]
    for copy in arrivals:
        copy.start()
    fields, steps = token_ids.shape
    ids = jnp.concatenate([widen(token_ids[...]), jnp.zeros((16 - fields, steps), F32)], axis=0)
    ids = ids.astype(BF16)
    for copy in arrivals:
        copy.wait()
    departures = []
    for pair in range(peers // 2):
        tiles = []
        for column in range(3):
            start = column * (wide // 3) + pair * LANES
            tile = widen(w_in[:, start : start + LANES])
            turned, first = halves(tile)
            tiles.append((tile, turned))
        first_half = first[:half]
        (zero, zero_turned), (one, one_turned), (two, two_turned) = tiles
        even, odd = 2 * pair, 2 * pair + 1
        packed[even, part_two, :] = jnp.where(first, zero, one_turned).astype(BF16)
        packed[odd, part_two, :] = jnp.where(first, zero_turned, one).astype(BF16)
        packed[even, part_one, :] = jnp.where(first_half, two[:half], two_turned[half:]).astype(
            BF16
        )
        packed[odd, part_one, :] = jnp.where(first_half, two_turned[:half], two[half:]).astype(
            BF16
        )
        turned = widen(cotangent[:, pair * LANES : (pair + 1) * LANES]).T.astype(BF16)
        packed[even, part_time, :] = turned[:rows]
        packed[odd, part_time, :] = turned[rows:]
        packed[even, part_ids, :] = ids
        packed[odd, part_ids, :] = ids
        both = pl.ds(even, 2)
        departures.append(
            pltpu.make_async_copy(packed.at[both], packed_far.at[both], sems.at[2 + pair])
        )
        departures[-1].start()
    for copy in departures:
        copy.wait()


def unpack_kernel(packed, mixer_out, weight_grads, tap_grads):
    peers = packed.shape[0]
    rows, wide = weight_grads.shape
    half = rows // 2
    part_two, part_one, part_time, part_taps = packed_parts(rows)
    for pair in range(peers // 2):
        even, odd = 2 * pair, 2 * pair + 1
        starts = [column * (wide // 3) + pair * LANES for column in range(3)]
        lanes = [slice(start, start + LANES) for start in starts]

        def merged(low, high):
            low_turned, first = halves(low)
            high_turned, _ = halves(high)
            return jnp.where(first, low, high_turned), jnp.where(first, low_turned, high)

        zero, one = merged(widen(packed[even, part_two, :]), widen(packed[odd, part_two, :]))
        weight_grads[:, lanes[0]] = zero
        weight_grads[:, lanes[1]] = one
        upper, lower = merged(widen(packed[even, part_one, :]), widen(packed[odd, part_one, :]))
        weight_grads[:half, lanes[2]] = upper
        weight_grads[half:, lanes[2]] = lower
        both = widen(jnp.concatenate([packed[even, part_time, :], packed[odd, part_time, :]], 0))
        mixer_out[:, pair * LANES : (pair + 1) * LANES] = both.T.astype(BF16)
        low = widen(packed[even, part_taps, :])
        high = widen(packed[odd, part_taps, :])
        low = low[:8] + low[8:]
        high = high[:8] + high[8:]
        zero, one = merged(low, high)
        tap_grads[:, lanes[0]] = zero[:3]
        tap_grads[:, lanes[1]] = one[:3]
        tap_grads[:, lanes[2]] = zero[3:6]


def mixer_kernel(packed_form, *refs):
    if packed_form:
        arrived, refs = refs[0], refs[1:]
        chans = refs[0].shape[0] // arrived.shape[0]
        part_two, part_one, part_time, part_small = packed_parts(chans)
        width = refs[0].shape[1]
        fields = refs[0].shape[0] // LANES
        two = widen(flat(arrived[:, part_two, :]))
        one = widen(arrived[:, part_one, :])
        one_turned = pltpu.roll(flat(one), LANES // 2, 1).reshape(one.shape)
        one = flat(jnp.concatenate([one, one_turned], axis=1))
        w_cols = jnp.concatenate([two, one], axis=1).astype(BF16)
        cotangent = arrived.at[:, part_time, :]

        def ids_of(block):
            return widen(arrived[block, part_small, :])[:fields]

    else:
        w_cols, ids, cotangent = refs[0][...], refs[1], refs[2]
        refs = refs[3:]
        chans = cotangent.shape[1]

        def ids_of(block):
            return widen(ids[block])

    far, refs = refs[:9], refs[9:]
    lagged_far, refs = refs[0], refs[1:]
    if packed_form:
        sent_far, refs = refs[0], refs[1:]
    else:
        (mixer_out, weight_part, tap_terms), refs = refs[:3], refs[3:]
    near, refs = refs[:9], refs[9:]
    sems, lagged_spec, hot, proj, mixed, grad_mixed, grad_proj = refs[:7]
    if packed_form:
        sent = refs[7]
        mixer_out = sent.at[:, part_time, :]
    entries, taps, filter_spec = near[:3]
    tables = near[3:]
    blocks = mixed.shape[0]
    codes = LANES
    arrivals = [
        pltpu.make_async_copy(source, target, sems.at[place])
        for place, (source, target) in enumerate(zip(far, near))
    ]
    for copy in arrivals:
        copy.start()
    departures = []

    def depart(source, target):
        departures.append(
            pltpu.make_async_copy(source, target, sems.at[len(arrivals) + len(departures)])
        )
        departures[-1].start()

    for block in range(blocks):
        hot[:, block * LANES : (block + 1) * LANES] = one_hot(ids_of(block), codes)
    arrivals[0].wait()
    coded = dot(entries[...], w_cols).T[: 3 * chans].astype(BF16)
    arrivals[1].wait()
    lane = lax.broadcasted_iota(jnp.int32, (3 * chans, LANES), 1)
    last1 = jnp.zeros((3 * chans, LANES), F32)
    last2 = last1
    for pair in range(blocks // 2):
        lanes = slice(2 * pair * LANES, (2 * pair + 2) * LANES)
        both = dot(coded, hot[:, lanes]).astype(BF16)
        for side in range(2):
            block = 2 * pair + side
            now = both[:, side * LANES : (side + 1) * LANES]
            proj[block] = now
            now = widen(now)
            turn1 = pltpu.roll(now, 1, 1)
            turn2 = pltpu.roll(now, 2, 1)
            late1 = jnp.where(lane < 1, last1, turn1)
            late2 = jnp.where(lane < 2, last2, turn2)
            last1, last2 = turn1, turn2
            mixed[block] = (taps[0] * now + taps[1] * late1 + taps[2] * late2).astype(BF16)

    def column(ref, group, place=0):
        return flat(ref[:, channel_rows(group, place * chans), :])

    def blocked(value):
        return value.reshape(blocks, GROUP, LANES)

    for copy in arrivals[2:]:
        copy.wait()
    for batch in batches(chans):
        value_spec = forward([column(mixed, group) for group in batch], tables)
        turned = [
            product(spectrum, filter_spec[0, group], False)
            for group, spectrum in zip(batch, value_spec)
        ]
        first_conv = [rounded(signal) for signal in inverse(turned, tables)]
        series = [
            (widen(column(mixed, group, 1)) * conv).astype(BF16)
            for group, conv in zip(batch, first_conv)
        ]
        mix_spec = forward(series, tables)
        turned = [
            product(spectrum, filter_spec[1, group], False)
            for group, spectrum in zip(batch, mix_spec)
        ]
        series = []
        for group, signal in zip(batch, inverse(turned, tables)):
            second_conv = rounded(signal)
            gate = widen(column(mixed, group, 2))
            upstream = widen(column(cotangent, group))
            mixer_out[:, channel_rows(group), :] = blocked((gate * second_conv).astype(BF16))
            grad_mixed[:, channel_rows(group, 2 * chans), :] = blocked(
                (upstream * second_conv).astype(BF16)
            )
            series.append((upstream * gate).astype(BF16))
        if packed_form:
            rows = pl.ds(part_time.start + batch[0] * GROUP, len(batch) * GROUP)
            depart(sent.at[:, rows, :], sent_far.at[:, rows, :])
        grad_spec = forward(series, tables)
        turned = []
        for place, group in enumerate(batch):
            lagged_spec[1, group] = product(grad_spec[place], mix_spec[place], True).astype(BF16)
            turned.append(product(grad_spec[place], filter_spec[1, group], True))
        series = []
        for place, signal in enumerate(inverse(turned, tables)):
            grad_mix = rounded(signal)
            group = batch[place]
            grad_mixed[:, channel_rows(group, chans), :] = blocked(
                (grad_mix * first_conv[place]).astype(BF16)
            )
            series.append((grad_mix * widen(column(mixed, group, 1))).astype(BF16))
        grad_spec = forward(series, tables)
        turned = []
        for place, group in enumerate(batch):
            lagged_spec[0, group] = product(grad_spec[place], value_spec[place], True).astype(BF16)
            turned.append(product(grad_spec[place], filter_spec[0, group], True))
        some = pl.ds(batch[0], len(batch))
        depart(lagged_spec.at[:, some], lagged_far.at[:, some])
        for group, signal in zip(batch, inverse(turned, tables)):
            grad_mixed[:, channel_rows(group), :] = blocked(signal.astype(BF16))

    next1 = jnp.zeros((3 * chans, LANES), F32)
    next2 = next1
    sums = [next1] * 3
    for block in reversed(range(blocks)):
        now = widen(grad_mixed[block])
        turn1 = pltpu.roll(now, LANES - 1, 1)
        turn2 = pltpu.roll(now, LANES - 2, 1)
        soon1 = jnp.where(lane >= LANES - 1, next1, turn1)
        soon2 = jnp.where(lane >= LANES - 2, next2, turn2)
        next1, next2 = turn1, turn2
        grad_proj[:, block * LANES : (block + 1) * LANES] = (
            taps[0] * now + taps[1] * soon1 + taps[2] * soon2
        ).astype(BF16)
        held = widen(proj[block])
        sums = [total + held * moved for total, moved in zip(sums, (now, soon1, soon2))]
    coded = lax.dot_general(
        grad_proj[...], hot[...], (((1,), (1,)), ((), ())), preferred_element_type=F32
    )
    weights = dot(coded.astype(BF16), entries[...])
    if not packed_form:
        weight_part[...] = weights.T.astype(BF16)
        for tap in range(3):
            tap_terms[tap] = jnp.sum(sums[tap], axis=1, keepdims=True)
        for copy in departures:
            copy.wait()
        return
    for tap in range(3):
        sums[tap] = jnp.sum(sums[tap].T, axis=0, keepdims=True)
    space = jnp.zeros((1, LANES), F32)
    total = jnp.concatenate(
        [sums[tap][:, :LANES] for tap in range(3)]
        + [
            jnp.concatenate([sums[tap][:, LANES:], space[:, : LANES - chans]], axis=1)
            for tap in range(3)
        ]
        + [space] * 2,
        axis=0,
    )
    high = rounded(total)
    small = jnp.concatenate([high, total - high], axis=0).astype(BF16)
    for block in range(blocks):
        sent[block, part_small, :] = small
    depart(sent.at[:, part_small, :], sent_far.at[:, part_small, :])
    two = weights[: 2 * chans].T
    sent[:, part_two, :] = two.astype(BF16).reshape(blocks, chans, LANES)
    depart(sent.at[:, part_two, :], sent_far.at[:, part_two, :])
    one = jnp.concatenate([weights[2 * chans :], jnp.zeros((LANES - chans, width), F32)], axis=0).T
    one = one.reshape(blocks, chans, LANES)
    half = chans // 2
    turned = pltpu.roll(flat(one[:, half:]), LANES // 2, 1)
    one = flat(one[:, :half])
    one = jnp.where(lax.broadcasted_iota(jnp.int32, one.shape, 1) < LANES // 2, one, turned)
    sent[:, part_one, :] = one.astype(BF16).reshape(blocks, half, LANES)
    depart(sent.at[:, part_one, :], sent_far.at[:, part_one, :])
    for copy in departures:
        copy.wait()


def lagged_kernel(lagged_spec, *rest):
    tables, filter_grads = rest[:6], rest[6]
    chans, steps = filter_grads.shape[1:]
    blocks = steps // LANES
    for which in range(2):
        for batch in batches(chans):
            turned = [lagged_spec[which, group] for group in batch]
            for group, signal in zip(batch, inverse(turned, tables)):
                for t in range(blocks):
                    filter_grads[which, channel_rows(group), t * LANES : (t + 1) * LANES] = signal[
                        t * GROUP : (t + 1) * GROUP
                    ]


def shape(dims, kind):
    return jax.ShapeDtypeStruct(dims, kind)


def exchange(blocks):
    return lax.all_to_all(blocks, "tm", split_axis=0, concat_axis=0, tiled=True)


def call(kernel, name, megabytes, **settings):
    return pl.pallas_call(
        kernel,
        name=name,
        compiler_params=pltpu.CompilerParams(vmem_limit_bytes=megabytes * 1024 * 1024),
        **settings,
    )


def send_inputs(token_ids, w_in, cotangent, peers):
    tok_rows, width = cotangent.shape
    rows, fields, chans = w_in.shape[0], token_ids.shape[1], width // peers
    w_send = w_in.reshape(rows, 3, peers, chans).transpose(2, 0, 1, 3)
    w_send = w_send.reshape(peers, rows * 3 * chans // LANES, LANES)
    ids_send = jnp.broadcast_to(token_ids.T.astype(BF16)[None], (peers, fields, tok_rows))
    cot_send = cotangent.T.reshape(peers, chans, tok_rows)
    arrived = exchange(jnp.concatenate([w_send, ids_send, cot_send], axis=1))
    count = w_send.shape[1]
    w_cols = arrived[:, :count].reshape(width, 3 * chans)
    return w_cols, arrived[:, count : count + fields], arrived[:, count + fields :]


def send_results(mixer_out, weight_part, tap_terms, peers, rows):
    _, chans, tok_rows = mixer_out.shape
    width = peers * chans
    count = 9 * chans
    tap_terms = tap_terms.reshape(1, count)
    tap_high = tap_terms.astype(BF16)
    tap_low = (tap_terms - widen(tap_high)).astype(BF16)
    tap_send = jnp.concatenate([tap_high, tap_low], axis=1)
    tap_send = jnp.pad(tap_send, ((0, 0), (0, -2 * count % LANES))).reshape(1, -1, LANES)
    tap_send = jnp.broadcast_to(tap_send, (peers,) + tap_send.shape[1:])
    weight_send = weight_part.reshape(peers, rows * 3 * chans // LANES, LANES)
    arrived = exchange(jnp.concatenate([mixer_out, weight_send, tap_send], axis=1))
    mixer_out = arrived[:, :chans].reshape(width, tok_rows).T
    place = chans + weight_send.shape[1]
    weight_grads = arrived[:, chans:place].reshape(peers, rows, 3, chans)
    weight_grads = widen(weight_grads).transpose(1, 2, 0, 3).reshape(rows, 3 * width)
    taps_moved = arrived[:, place:].reshape(peers, -1)
    tap_grads = widen(taps_moved[:, :count]) + widen(taps_moved[:, count : 2 * count])
    tap_grads = tap_grads.reshape(peers, 3, 3, chans).transpose(1, 2, 0, 3)
    return mixer_out, weight_grads, tap_grads.reshape(3, 3 * width)


def local(token_ids, field_offsets, embed_table, w_in, short_taps, filters, cotangent):
    tok_rows, width = cotangent.shape
    peers = lax.axis_size("tm")
    fields = token_ids.shape[1]
    rows = w_in.shape[0]
    chans = width // peers
    steps = tok_rows * peers
    groups = chans // GROUP
    tables = transform_tables(peers)
    packed_form = 2 * chans == LANES and rows == chans and fields <= 8
    spec = (2, groups, peers * GROUP, 2 * LANES)
    moved = (peers, chans, LANES)
    wide = (peers, 3 * chans, LANES)
    packed = shape((peers, packed_parts(rows)[-1].stop, LANES), BF16)

    near = pl.BlockSpec(memory_space=pltpu.VMEM)
    far = pl.BlockSpec(memory_space=pltpu.HBM)

    if packed_form:
        sent = call(
            pack_kernel,
            "pack",
            16,
            in_specs=[near, far, far],
            out_specs=far,
            out_shape=packed,
            scratch_shapes=[
                pltpu.VMEM(w_in.shape, BF16),
                pltpu.VMEM(cotangent.shape, BF16),
                pltpu.VMEM(packed.shape, BF16),
                pltpu.SemaphoreType.DMA((2 + peers // 2,)),
            ],
        )(token_ids.T, w_in, cotangent)
        arrived = (exchange(sent),)
    else:
        arrived = send_inputs(token_ids, w_in, cotangent, peers)

    filter_spec, entries = call(
        prepare_kernel,
        "prepare",
        32,
        in_specs=[pl.BlockSpec(memory_space=pltpu.SMEM)] + [near] * 8,
        out_shape=(shape(spec, F32), shape(embed_table.shape, BF16)),
        cost_estimate=pl.CostEstimate(
            flops=10**10, bytes_accessed=3 * 10**7, transcendentals=0
        ),
    )(field_offsets, filters, embed_table, *tables)
    taps = short_taps.reshape(3, 3, peers, chans)
    taps = lax.dynamic_index_in_dim(taps, lax.axis_index("tm"), axis=2, keepdims=False)
    taps = jnp.broadcast_to(taps.reshape(3, 3 * chans, 1), (3, 3 * chans, LANES))

    if packed_form:
        out_shape = (shape(spec, BF16), packed)
        out_specs = (far, far)
        scratch_shapes = [pltpu.VMEM(packed.shape, BF16)]
    else:
        out_shape = (
            shape(spec, BF16),
            shape(moved, BF16),
            shape((width, 3 * chans), BF16),
            shape((3, 3 * chans, 1), F32),
        )
        out_specs = (far, near, near, near)
        scratch_shapes = []
    operands = (entries, taps, filter_spec) + tables
    hot_bytes = 2 * embed_table.shape[0] * steps
    results = call(
        functools.partial(mixer_kernel, packed_form),
        "mixer",
        20 + 2 * hot_bytes // 2**20,
        in_specs=[near] * len(arrived) + [far] * len(operands),
        out_shape=out_shape,
        out_specs=out_specs,
        scratch_shapes=[pltpu.VMEM(operand.shape, operand.dtype) for operand in operands]
        + [
            pltpu.SemaphoreType.DMA((len(operands) + 2 * groups + 3,)),
            pltpu.VMEM(spec, BF16),
            pltpu.VMEM((embed_table.shape[0], steps), BF16),
            pltpu.VMEM(wide, BF16),
            pltpu.VMEM(wide, BF16),
            pltpu.VMEM(wide, BF16),
            pltpu.VMEM((3 * chans, steps), BF16),
        ]
        + scratch_shapes,
    )(*arrived, *operands)
    filter_grads = call(
        lagged_kernel,
        "lagged",
        24,
        out_shape=shape((2, chans, steps), F32),
        cost_estimate=pl.CostEstimate(
            flops=10**10, bytes_accessed=3 * 10**7, transcendentals=0
        ),
    )(results[0], *tables)
    if packed_form:
        mixer_out, weight_grads, tap_grads = call(
            unpack_kernel,
            "unpack",
            16,
            out_shape=(
                shape((tok_rows, width), BF16),
                shape((rows, 3 * width), F32),
                shape((3, 3 * width), F32),
            ),
        )(exchange(results[1]))
    else:
        mixer_out, weight_grads, tap_grads = send_results(*results[1:], peers, rows)
    return (mixer_out, weight_grads, tap_grads, filter_grads)


def solution(mesh):
    return jax.shard_map(
        local,
        mesh=mesh,
        in_specs=(
            P(("groups", "tm"), None),
            P("groups"),
            P(),
            P("tm", None),
            P(),
            P(None, "tm", None),
            P(("groups", "tm"), None),
        ),
        out_specs=(
            P(("groups", "tm"), None),
            P(("groups", "tm"), None),
            P("groups", None),
            P("groups", "tm", None),
        ),
        check_vma=False,
    )
```

```python
import functools
import math


import jax
import jax.numpy as jnp
import ml_dtypes
import numpy as np
from jax import lax
from jax.experimental import pallas as pl
from jax.experimental.pallas import tpu as pltpu
from jax.sharding import PartitionSpec as P

F32 = jnp.float32
BF16 = jnp.bfloat16
LANES = 128
GROUP = 16
PACK_MB = 62
MIX_MB = 61.5


def widen(array):
    return array.astype(F32)


def rounded(array):
    return array.astype(BF16).astype(F32)


def transform_tables(blocks):
    total = 2 * blocks * LANES
    row = np.arange(blocks) + 0.5
    first = np.exp(-2j * np.pi * np.outer(row, np.arange(blocks)) / (2 * blocks))
    turn = np.exp(-2j * np.pi * np.outer(row, np.arange(LANES)) / total)
    second = np.exp(-2j * np.pi * np.outer(np.arange(LANES), np.arange(LANES)) / LANES)
    same = np.eye(GROUP)
    first_rows = np.concatenate([first.real, first.imag], axis=0)
    back_rows = np.concatenate([first.real.T, first.imag.T], axis=1) * (2.0 / total)
    forward = np.block([[second.real, second.imag], [-second.imag, second.real]])
    inverse = np.block([[second.real, -second.imag], [second.imag, second.real]])
    narrow = ml_dtypes.bfloat16
    return (
        np.kron(first_rows, same).astype(narrow),
        np.kron(back_rows, same).astype(narrow),
        forward.astype(narrow),
        inverse.astype(narrow),
        np.repeat(turn.real, GROUP, axis=0).astype(np.float32),
        np.repeat(turn.imag, GROUP, axis=0).astype(np.float32),
    )


def dot(left, right):
    return jnp.dot(left, right, preferred_element_type=F32)


def joined(parts, axis):
    return parts[0] if len(parts) == 1 else jnp.concatenate(parts, axis=axis)


def forward(series, tables):
    first, _, second, _, turn_re, turn_im = tables
    rows = turn_re.shape[0]
    part = dot(first[...], joined(series, 1))
    spectra = []
    for place in range(len(series)):
        lanes = slice(place * LANES, (place + 1) * LANES)
        part_re = part[:rows, lanes]
        part_im = part[rows:, lanes]
        turned = jnp.concatenate(
            [
                part_re * turn_re[...] - part_im * turn_im[...],
                part_re * turn_im[...] + part_im * turn_re[...],
            ],
            axis=1,
        )
        spectra.append(dot(turned.astype(BF16), second[...]))
    return spectra


def inverse(spectra, tables):
    _, last, _, second, turn_re, turn_im = tables
    turned = []
    for spectrum in spectra:
        back = dot(spectrum.astype(BF16), second[...])
        back_re = back[:, :LANES]
        back_im = back[:, LANES:]
        turned.append(
            jnp.concatenate(
                [
                    back_re * turn_re[...] + back_im * turn_im[...],
                    back_im * turn_re[...] - back_re * turn_im[...],
                ],
                axis=0,
            ).astype(BF16)
        )
    signal = dot(last[...], joined(turned, 1))
    return [signal[:, place * LANES : (place + 1) * LANES] for place in range(len(spectra))]


def product(left, right, conjugate):
    left_re, left_im = left[:, :LANES], left[:, LANES:]
    right_re, right_im = right[:, :LANES], right[:, LANES:]
    if conjugate:
        return jnp.concatenate(
            [
                left_re * right_re + left_im * right_im,
                left_im * right_re - left_re * right_im,
            ],
            axis=1,
        )
    return jnp.concatenate(
        [
            left_re * right_re - left_im * right_im,
            left_re * right_im + left_im * right_re,
        ],
        axis=1,
    )


def batches(chans):
    groups = chans // GROUP
    size = math.gcd(groups, 4)
    return [range(start, start + size) for start in range(0, groups, size)]


def channel_rows(group, offset=0):
    return slice(offset + group * GROUP, offset + (group + 1) * GROUP)


def flat(block):
    return block.reshape(block.shape[0] * block.shape[1], block.shape[2])


def one_hot(ids, codes):
    fields, lanes = ids.shape
    code = lax.broadcasted_iota(jnp.int32, (codes, lanes), 0).astype(F32).astype(BF16)
    one, zero = jnp.ones((codes, lanes), BF16), jnp.zeros((codes, lanes), BF16)
    return jnp.concatenate(
        [jnp.where(code == ids[field : field + 1], one, zero) for field in range(fields)],
        axis=0,
    )


def prepare_kernel(offsets, filters, table, short_taps, *rest):
    tables = rest[:6]
    spectra, entries, taps = rest[6:]
    taps[...] = jnp.broadcast_to(short_taps[...], taps.shape)
    chans, steps = filters.shape[1:]
    blocks = steps // LANES
    fields = offsets.shape[0]
    codes = entries.shape[0] // fields
    window = codes + GROUP
    for field in range(fields):
        start = jnp.minimum(offsets[field] // GROUP * GROUP, table.shape[0] - window)
        row = lax.broadcasted_iota(jnp.int32, (codes, window), 0) + (offsets[field] - start)
        place = lax.broadcasted_iota(jnp.int32, (codes, window), 1)
        picked = jnp.where(row == place, 1.0, 0.0).astype(BF16)
        entries[field * codes : (field + 1) * codes, :] = dot(
            picked, table[pl.ds(pl.multiple_of(start, GROUP), window), :]
        ).astype(BF16)
    for which in range(2):
        for batch in batches(chans):
            series = [
                jnp.concatenate(
                    [
                        filters[which, channel_rows(group), t * LANES : (t + 1) * LANES]
                        for t in range(blocks)
                    ],
                    axis=0,
                )
                for group in batch
            ]
            for group, spectrum in zip(batch, forward(series, tables)):
                spectra[which, group] = spectrum


def halves(array):
    lane = lax.broadcasted_iota(jnp.int32, array.shape, 1)
    return pltpu.roll(array, LANES // 2, 1), lane < LANES // 2


def packed_parts(rows):
    half = rows // 2
    marks = [0, rows, rows + half, 2 * rows + half, 2 * rows + half + 8]
    return [slice(low, high) for low, high in zip(marks[:-1], marks[1:])]


def pack_kernel(token_ids, w_in_far, cotangent_far, packed_far, w_in, cotangent, packed, sems):
    peers = packed.shape[0]
    rows, wide = w_in.shape
    half = rows // 2
    part_two, part_one, part_time, part_ids = packed_parts(rows)
    arrivals = [
        pltpu.make_async_copy(far, near, sems.at[place])
        for place, (far, near) in enumerate(((w_in_far, w_in), (cotangent_far, cotangent)))
    ]
    for copy in arrivals:
        copy.start()
    ids = widen(token_ids[...]).astype(BF16)
    for copy in arrivals:
        copy.wait()
    departures = []
    for pair in range(peers // 2):
        tiles = []
        for column in range(3):
            start = column * (wide // 3) + pair * LANES
            tile = widen(w_in[:, start : start + LANES])
            turned, first = halves(tile)
            tiles.append((tile, turned))
        first_half = first[:half]
        (zero, zero_turned), (one, one_turned), (two, two_turned) = tiles
        even, odd = 2 * pair, 2 * pair + 1
        packed[even, part_two, :] = jnp.where(first, zero, one_turned).astype(BF16)
        packed[odd, part_two, :] = jnp.where(first, zero_turned, one).astype(BF16)
        packed[even, part_one, :] = jnp.where(first_half, two[:half], two_turned[half:]).astype(
            BF16
        )
        packed[odd, part_one, :] = jnp.where(first_half, two_turned[:half], two[half:]).astype(
            BF16
        )
        turned = widen(cotangent[:, pair * LANES : (pair + 1) * LANES]).T.astype(BF16)
        packed[even, part_time, :] = turned[:rows]
        packed[odd, part_time, :] = turned[rows:]
        packed[even, part_ids, :] = ids
        packed[odd, part_ids, :] = ids
        both = pl.ds(even, 2)
        departures.append(
            pltpu.make_async_copy(packed.at[both], packed_far.at[both], sems.at[2 + pair])
        )
        departures[-1].start()
    for copy in departures:
        copy.wait()


def unpack_kernel(packed, mixer_out, weight_grads, tap_grads):
    peers = packed.shape[0]
    rows, wide = weight_grads.shape
    half = rows // 2
    part_two, part_one, part_time, part_taps = packed_parts(rows)
    for pair in range(peers // 2):
        even, odd = 2 * pair, 2 * pair + 1
        starts = [column * (wide // 3) + pair * LANES for column in range(3)]
        lanes = [slice(start, start + LANES) for start in starts]

        def merged(low, high):
            low_turned, first = halves(low)
            high_turned, _ = halves(high)
            return jnp.where(first, low, high_turned), jnp.where(first, low_turned, high)

        zero, one = merged(widen(packed[even, part_two, :]), widen(packed[odd, part_two, :]))
        weight_grads[:, lanes[0]] = zero
        weight_grads[:, lanes[1]] = one
        upper, lower = merged(widen(packed[even, part_one, :]), widen(packed[odd, part_one, :]))
        weight_grads[:half, lanes[2]] = upper
        weight_grads[half:, lanes[2]] = lower
        both = widen(jnp.concatenate([packed[even, part_time, :], packed[odd, part_time, :]], 0))
        mixer_out[:, pair * LANES : (pair + 1) * LANES] = both.T.astype(BF16)
        low = widen(packed[even, part_taps, :])
        high = widen(packed[odd, part_taps, :])
        zero, one = merged(low, high)
        tap_grads[:, lanes[0]] = zero[:3]
        tap_grads[:, lanes[1]] = one[:3]
        tap_grads[:, lanes[2]] = zero[3:6]


def mixer_kernel(packed_form, *refs):
    if packed_form:
        arrived, refs = refs[0], refs[1:]
        chans = refs[0].shape[0] // arrived.shape[0]
        part_two, part_one, part_time, part_small = packed_parts(chans)
        width = refs[0].shape[1]
        two = widen(flat(arrived[:, part_two, :]))
        one = widen(arrived[:, part_one, :])
        one_turned = pltpu.roll(flat(one), LANES // 2, 1).reshape(one.shape)
        one = flat(jnp.concatenate([one, one_turned], axis=1))
        w_cols = jnp.concatenate([two, one], axis=1).astype(BF16)
        cotangent = arrived.at[:, part_time, :]

        def ids_of(block):
            return arrived[block, part_small, :]

    else:
        w_cols, ids, cotangent = refs[0][...], refs[1], refs[2]
        refs = refs[3:]
        chans = cotangent.shape[1]

        def ids_of(block):
            return ids[block]

    far, refs = refs[:9], refs[9:]
    lagged_far, refs = refs[0], refs[1:]
    if packed_form:
        sent_far, refs = refs[0], refs[1:]
    else:
        (mixer_out, weight_part, tap_terms), refs = refs[:3], refs[3:]
    near, refs = refs[:9], refs[9:]
    sems, lagged_spec, hot, proj, mixed, grad_mixed, grad_proj = refs[:7]
    if packed_form:
        sent = refs[7]
        mixer_out = sent.at[:, part_time, :]
    entries, taps, filter_spec = near[:3]
    tables = near[3:]
    blocks = mixed.shape[0]
    codes = LANES
    arrivals = [
        pltpu.make_async_copy(source, target, sems.at[place])
        for place, (source, target) in enumerate(zip(far, near))
    ]
    for copy in arrivals:
        copy.start()
    departures = []

    def depart(source, target):
        departures.append(
            pltpu.make_async_copy(source, target, sems.at[len(arrivals) + len(departures)])
        )
        departures[-1].start()

    for block in range(blocks):
        hot[:, block * LANES : (block + 1) * LANES] = one_hot(ids_of(block), codes)
    arrivals[0].wait()
    coded = dot(entries[...], w_cols).T[: 3 * chans].astype(BF16)
    arrivals[1].wait()
    lane = lax.broadcasted_iota(jnp.int32, (3 * chans, LANES), 1)
    last1 = jnp.zeros((3 * chans, LANES), F32)
    last2 = last1
    for pair in range(blocks // 2):
        lanes = slice(2 * pair * LANES, (2 * pair + 2) * LANES)
        both = dot(coded, hot[:, lanes]).astype(BF16)
        for side in range(2):
            block = 2 * pair + side
            now = both[:, side * LANES : (side + 1) * LANES]
            proj[block] = now
            now = widen(now)
            turn1 = pltpu.roll(now, 1, 1)
            turn2 = pltpu.roll(now, 2, 1)
            late1 = jnp.where(lane < 1, last1, turn1)
            late2 = jnp.where(lane < 2, last2, turn2)
            last1, last2 = turn1, turn2
            mixed[block] = (taps[0] * now + taps[1] * late1 + taps[2] * late2).astype(BF16)

    def column(ref, group, place=0):
        return flat(ref[:, channel_rows(group, place * chans), :])

    def blocked(value):
        return value.reshape(blocks, GROUP, LANES)

    for copy in arrivals[2:]:
        copy.wait()
    for batch in batches(chans):
        value_spec = forward([column(mixed, group) for group in batch], tables)
        turned = [
            product(spectrum, filter_spec[0, group], False)
            for group, spectrum in zip(batch, value_spec)
        ]
        first_conv = [rounded(signal) for signal in inverse(turned, tables)]
        series = [
            (widen(column(mixed, group, 1)) * conv).astype(BF16)
            for group, conv in zip(batch, first_conv)
        ]
        mix_spec = forward(series, tables)
        turned = [
            product(spectrum, filter_spec[1, group], False)
            for group, spectrum in zip(batch, mix_spec)
        ]
        series = []
        for group, signal in zip(batch, inverse(turned, tables)):
            second_conv = rounded(signal)
            gate = widen(column(mixed, group, 2))
            upstream = widen(column(cotangent, group))
            mixer_out[:, channel_rows(group), :] = blocked((gate * second_conv).astype(BF16))
            grad_mixed[:, channel_rows(group, 2 * chans), :] = blocked(
                (upstream * second_conv).astype(BF16)
            )
            series.append((upstream * gate).astype(BF16))
        grad_spec = forward(series, tables)
        turned = []
        for place, group in enumerate(batch):
            lagged_spec[1, group] = product(grad_spec[place], mix_spec[place], True).astype(BF16)
            turned.append(product(grad_spec[place], filter_spec[1, group], True))
        series = []
        for place, signal in enumerate(inverse(turned, tables)):
            grad_mix = rounded(signal)
            group = batch[place]
            grad_mixed[:, channel_rows(group, chans), :] = blocked(
                (grad_mix * first_conv[place]).astype(BF16)
            )
            series.append((grad_mix * widen(column(mixed, group, 1))).astype(BF16))
        grad_spec = forward(series, tables)
        turned = []
        for place, group in enumerate(batch):
            lagged_spec[0, group] = product(grad_spec[place], value_spec[place], True).astype(BF16)
            turned.append(product(grad_spec[place], filter_spec[0, group], True))
        some = pl.ds(batch[0], len(batch))
        depart(lagged_spec.at[:, some], lagged_far.at[:, some])
        for group, signal in zip(batch, inverse(turned, tables)):
            grad_mixed[:, channel_rows(group), :] = blocked(signal.astype(BF16))

    next1 = jnp.zeros((3 * chans, LANES), F32)
    next2 = next1
    sums = [next1] * 3
    for block in reversed(range(blocks)):
        now = widen(grad_mixed[block])
        turn1 = pltpu.roll(now, LANES - 1, 1)
        turn2 = pltpu.roll(now, LANES - 2, 1)
        soon1 = jnp.where(lane >= LANES - 1, next1, turn1)
        soon2 = jnp.where(lane >= LANES - 2, next2, turn2)
        next1, next2 = turn1, turn2
        grad_proj[:, block * LANES : (block + 1) * LANES] = (
            taps[0] * now + taps[1] * soon1 + taps[2] * soon2
        ).astype(BF16)
        held = widen(proj[block])
        sums = [total + held * moved for total, moved in zip(sums, (now, soon1, soon2))]
    coded = lax.dot_general(
        grad_proj[...], hot[...], (((1,), (1,)), ((), ())), preferred_element_type=F32
    )
    weights = dot(coded.astype(BF16), entries[...])
    if not packed_form:
        weight_part[...] = weights.T.astype(BF16)
        for tap in range(3):
            tap_terms[tap] = jnp.sum(sums[tap], axis=1, keepdims=True)
        for copy in departures:
            copy.wait()
        return
    for tap in range(3):
        sums[tap] = jnp.sum(sums[tap].T, axis=0, keepdims=True)
    space = jnp.zeros((1, LANES), F32)
    total = jnp.concatenate(
        [sums[tap][:, :LANES] for tap in range(3)]
        + [
            jnp.concatenate([sums[tap][:, LANES:], space[:, : LANES - chans]], axis=1)
            for tap in range(3)
        ]
        + [space] * 2,
        axis=0,
    )
    for block in range(blocks):
        sent[block, part_small, :] = total.astype(BF16)
    two = weights[: 2 * chans].T
    sent[:, part_two, :] = two.astype(BF16).reshape(blocks, chans, LANES)
    one = jnp.concatenate([weights[2 * chans :], jnp.zeros((LANES - chans, width), F32)], axis=0).T
    one = one.reshape(blocks, chans, LANES)
    half = chans // 2
    turned = pltpu.roll(flat(one[:, half:]), LANES // 2, 1)
    one = flat(one[:, :half])
    one = jnp.where(lax.broadcasted_iota(jnp.int32, one.shape, 1) < LANES // 2, one, turned)
    sent[:, part_one, :] = one.astype(BF16).reshape(blocks, half, LANES)
    depart(sent, sent_far)
    for copy in departures:
        copy.wait()


def lagged_kernel(lagged_spec, *rest):
    tables, filter_grads = rest[:6], rest[6]
    chans, steps = filter_grads.shape[1:]
    blocks = steps // LANES
    for which in range(2):
        for batch in batches(chans):
            turned = [lagged_spec[which, group] for group in batch]
            for group, signal in zip(batch, inverse(turned, tables)):
                for t in range(blocks):
                    filter_grads[which, channel_rows(group), t * LANES : (t + 1) * LANES] = signal[
                        t * GROUP : (t + 1) * GROUP
                    ]


def shape(dims, kind):
    return jax.ShapeDtypeStruct(dims, kind)


def exchange(blocks):
    return lax.all_to_all(blocks, "tm", split_axis=0, concat_axis=0, tiled=True)


def call(kernel, name, megabytes, **settings):
    return pl.pallas_call(
        kernel,
        name=name,
        compiler_params=pltpu.CompilerParams(vmem_limit_bytes=int(megabytes * 1024 * 1024)),
        **settings,
    )


def send_inputs(token_ids, w_in, cotangent, peers):
    tok_rows, width = cotangent.shape
    rows, fields, chans = w_in.shape[0], token_ids.shape[1], width // peers
    w_send = w_in.reshape(rows, 3, peers, chans).transpose(2, 0, 1, 3)
    w_send = w_send.reshape(peers, rows * 3 * chans // LANES, LANES)
    ids_send = jnp.broadcast_to(token_ids.T.astype(BF16)[None], (peers, fields, tok_rows))
    cot_send = cotangent.T.reshape(peers, chans, tok_rows)
    arrived = exchange(jnp.concatenate([w_send, ids_send, cot_send], axis=1))
    count = w_send.shape[1]
    w_cols = arrived[:, :count].reshape(width, 3 * chans)
    return w_cols, arrived[:, count : count + fields], arrived[:, count + fields :]


def send_results(mixer_out, weight_part, tap_terms, peers, rows):
    _, chans, tok_rows = mixer_out.shape
    width = peers * chans
    count = 9 * chans
    tap_terms = tap_terms.reshape(1, count)
    tap_high = tap_terms.astype(BF16)
    tap_low = (tap_terms - widen(tap_high)).astype(BF16)
    tap_send = jnp.concatenate([tap_high, tap_low], axis=1)
    tap_send = jnp.pad(tap_send, ((0, 0), (0, -2 * count % LANES))).reshape(1, -1, LANES)
    tap_send = jnp.broadcast_to(tap_send, (peers,) + tap_send.shape[1:])
    weight_send = weight_part.reshape(peers, rows * 3 * chans // LANES, LANES)
    arrived = exchange(jnp.concatenate([mixer_out, weight_send, tap_send], axis=1))
    mixer_out = arrived[:, :chans].reshape(width, tok_rows).T
    place = chans + weight_send.shape[1]
    weight_grads = arrived[:, chans:place].reshape(peers, rows, 3, chans)
    weight_grads = widen(weight_grads).transpose(1, 2, 0, 3).reshape(rows, 3 * width)
    taps_moved = arrived[:, place:].reshape(peers, -1)
    tap_grads = widen(taps_moved[:, :count]) + widen(taps_moved[:, count : 2 * count])
    tap_grads = tap_grads.reshape(peers, 3, 3, chans).transpose(1, 2, 0, 3)
    return mixer_out, weight_grads, tap_grads.reshape(3, 3 * width)


def local(token_ids, field_offsets, embed_table, w_in, short_taps, filters, cotangent):
    tok_rows, width = cotangent.shape
    peers = lax.axis_size("tm")
    fields = token_ids.shape[1]
    rows = w_in.shape[0]
    chans = width // peers
    steps = tok_rows * peers
    groups = chans // GROUP
    tables = transform_tables(peers)
    packed_form = 2 * chans == LANES and rows == chans and fields == 8
    spec = (2, groups, peers * GROUP, 2 * LANES)
    moved = (peers, chans, LANES)
    wide = (peers, 3 * chans, LANES)
    packed = shape((peers, packed_parts(rows)[-1].stop, LANES), BF16)

    near = pl.BlockSpec(memory_space=pltpu.VMEM)
    far = pl.BlockSpec(memory_space=pltpu.HBM)

    if packed_form:
        sent = call(
            pack_kernel,
            "pack",
            PACK_MB,
            in_specs=[near, far, far],
            out_specs=far,
            out_shape=packed,
            scratch_shapes=[
                pltpu.VMEM(w_in.shape, BF16),
                pltpu.VMEM(cotangent.shape, BF16),
                pltpu.VMEM(packed.shape, BF16),
                pltpu.SemaphoreType.DMA((2 + peers // 2,)),
            ],
        )(token_ids.T, w_in, cotangent)
        arrived = (exchange(sent),)
    else:
        arrived = send_inputs(token_ids, w_in, cotangent, peers)

    taps = short_taps.reshape(3, 3, peers, chans)
    taps = lax.dynamic_index_in_dim(taps, lax.axis_index("tm"), axis=2, keepdims=False)
    filter_spec, entries, taps = call(
        prepare_kernel,
        "prepare",
        32,
        in_specs=[pl.BlockSpec(memory_space=pltpu.SMEM)] + [near] * 9,
        out_shape=(
            shape(spec, F32),
            shape(embed_table.shape, BF16),
            shape((3, 3 * chans, LANES), F32),
        ),
        cost_estimate=pl.CostEstimate(
            flops=10**10, bytes_accessed=3 * 10**7, transcendentals=0
        ),
    )(field_offsets, filters, embed_table, taps.reshape(3, 3 * chans, 1), *tables)
    if packed_form:
        out_shape = (shape(spec, BF16), packed)
        out_specs = (far, far)
        scratch_shapes = [pltpu.VMEM(packed.shape, BF16)]
    else:
        out_shape = (
            shape(spec, BF16),
            shape(moved, BF16),
            shape((width, 3 * chans), BF16),
            shape((3, 3 * chans, 1), F32),
        )
        out_specs = (far, near, near, near)
        scratch_shapes = []
    operands = (entries, taps, filter_spec) + tables
    results = call(
        functools.partial(mixer_kernel, packed_form),
        "mixer",
        MIX_MB,
        in_specs=[near] * len(arrived) + [far] * len(operands),
        out_shape=out_shape,
        out_specs=out_specs,
        scratch_shapes=[pltpu.VMEM(operand.shape, operand.dtype) for operand in operands]
        + [
            pltpu.SemaphoreType.DMA((len(operands) + groups + 1,)),
            pltpu.VMEM(spec, BF16),
            pltpu.VMEM((embed_table.shape[0], steps), BF16),
            pltpu.VMEM(wide, BF16),
            pltpu.VMEM(wide, BF16),
            pltpu.VMEM(wide, BF16),
            pltpu.VMEM((3 * chans, steps), BF16),
        ]
        + scratch_shapes,
    )(*arrived, *operands)
    filter_grads = call(
        lagged_kernel,
        "lagged",
        24,
        out_shape=shape((2, chans, steps), F32),
        cost_estimate=pl.CostEstimate(
            flops=10**10, bytes_accessed=3 * 10**7, transcendentals=0
        ),
    )(results[0], *tables)
    if packed_form:
        mixer_out, weight_grads, tap_grads = call(
            unpack_kernel,
            "unpack",
            16,
            out_shape=(
                shape((tok_rows, width), BF16),
                shape((rows, 3 * width), F32),
                shape((3, 3 * width), F32),
            ),
        )(exchange(results[1]))
    else:
        mixer_out, weight_grads, tap_grads = send_results(*results[1:], peers, rows)
    return (mixer_out, weight_grads, tap_grads, filter_grads)


def solution(mesh):
    return jax.shard_map(
        local,
        mesh=mesh,
        in_specs=(
            P(("groups", "tm"), None),
            P("groups"),
            P(),
            P("tm", None),
            P(),
            P(None, "tm", None),
            P(("groups", "tm"), None),
        ),
        out_specs=(
            P(("groups", "tm"), None),
            P(("groups", "tm"), None),
            P("groups", None),
            P("groups", "tm", None),
        ),
        check_vma=False,
    )
```

```python
import functools
import math


import jax
import jax.numpy as jnp
import ml_dtypes
import numpy as np
from jax import lax
from jax.experimental import pallas as pl
from jax.experimental.pallas import tpu as pltpu
from jax.sharding import PartitionSpec as P

F32 = jnp.float32
BF16 = jnp.bfloat16
LANES = 128
GROUP = 16
QUARTERS = 2
PACK_MB = 62
MIX_MB = 61.5


def widen(array):
    return array.astype(F32)


def rounded(array):
    return array.astype(BF16).astype(F32)


def transform_tables(blocks):
    total = 2 * blocks * LANES
    row = np.arange(blocks) + 0.5
    first = np.exp(-2j * np.pi * np.outer(row, np.arange(blocks)) / (2 * blocks))
    turn = np.exp(-2j * np.pi * np.outer(row, np.arange(LANES)) / total)
    second = np.exp(-2j * np.pi * np.outer(np.arange(LANES), np.arange(LANES)) / LANES)
    same = np.eye(GROUP)
    first_rows = np.concatenate([first.real, first.imag], axis=0)
    back_rows = np.concatenate([first.real.T, first.imag.T], axis=1) * (2.0 / total)
    forward = np.block([[second.real, second.imag], [-second.imag, second.real]])
    inverse = np.block([[second.real, -second.imag], [second.imag, second.real]])
    narrow = ml_dtypes.bfloat16
    return (
        np.kron(first_rows, same).astype(narrow),
        np.kron(back_rows, same).astype(narrow),
        forward.astype(narrow),
        inverse.astype(narrow),
        np.repeat(turn.real, GROUP, axis=0).astype(np.float32),
        np.repeat(turn.imag, GROUP, axis=0).astype(np.float32),
    )


def dot(left, right):
    return jnp.dot(left, right, preferred_element_type=F32)


def joined(parts, axis):
    return parts[0] if len(parts) == 1 else jnp.concatenate(parts, axis=axis)


def forward(series, tables):
    first, _, second, _, turn_re, turn_im = tables
    rows = turn_re.shape[0]
    part = dot(first[...], joined(series, 1))
    spectra = []
    for place in range(len(series)):
        lanes = slice(place * LANES, (place + 1) * LANES)
        part_re = part[:rows, lanes]
        part_im = part[rows:, lanes]
        turned = jnp.concatenate(
            [
                part_re * turn_re[...] - part_im * turn_im[...],
                part_re * turn_im[...] + part_im * turn_re[...],
            ],
            axis=1,
        )
        spectra.append(dot(turned.astype(BF16), second[...]))
    return spectra


def inverse(spectra, tables):
    _, last, _, second, turn_re, turn_im = tables
    turned = []
    for spectrum in spectra:
        back = dot(spectrum.astype(BF16), second[...])
        back_re = back[:, :LANES]
        back_im = back[:, LANES:]
        turned.append(
            jnp.concatenate(
                [
                    back_re * turn_re[...] + back_im * turn_im[...],
                    back_im * turn_re[...] - back_re * turn_im[...],
                ],
                axis=0,
            ).astype(BF16)
        )
    signal = dot(last[...], joined(turned, 1))
    return [signal[:, place * LANES : (place + 1) * LANES] for place in range(len(spectra))]


def product(left, right, conjugate):
    left_re, left_im = left[:, :LANES], left[:, LANES:]
    right_re, right_im = right[:, :LANES], right[:, LANES:]
    if conjugate:
        return jnp.concatenate(
            [
                left_re * right_re + left_im * right_im,
                left_im * right_re - left_re * right_im,
            ],
            axis=1,
        )
    return jnp.concatenate(
        [
            left_re * right_re - left_im * right_im,
            left_re * right_im + left_im * right_re,
        ],
        axis=1,
    )


def batches(chans):
    groups = chans // GROUP
    size = math.gcd(groups, 4)
    return [range(start, start + size) for start in range(0, groups, size)]


def channel_rows(group, offset=0):
    return slice(offset + group * GROUP, offset + (group + 1) * GROUP)


def flat(block):
    return block.reshape(block.shape[0] * block.shape[1], block.shape[2])


def one_hot(ids, codes):
    fields, lanes = ids.shape
    code = lax.broadcasted_iota(jnp.int32, (codes, lanes), 0).astype(F32).astype(BF16)
    one, zero = jnp.ones((codes, lanes), BF16), jnp.zeros((codes, lanes), BF16)
    return jnp.concatenate(
        [jnp.where(code == ids[field : field + 1], one, zero) for field in range(fields)],
        axis=0,
    )


def prepare_kernel(offsets, filters, table, short_taps, *rest):
    tables = rest[:6]
    spectra, entries, taps = rest[6:]
    taps[...] = jnp.broadcast_to(short_taps[...], taps.shape)
    chans, steps = filters.shape[1:]
    blocks = steps // LANES
    fields = offsets.shape[0]
    codes = entries.shape[0] // fields
    window = codes + GROUP
    for field in range(fields):
        start = jnp.minimum(offsets[field] // GROUP * GROUP, table.shape[0] - window)
        row = lax.broadcasted_iota(jnp.int32, (codes, window), 0) + (offsets[field] - start)
        place = lax.broadcasted_iota(jnp.int32, (codes, window), 1)
        picked = jnp.where(row == place, 1.0, 0.0).astype(BF16)
        entries[field * codes : (field + 1) * codes, :] = dot(
            picked, table[pl.ds(pl.multiple_of(start, GROUP), window), :]
        ).astype(BF16)
    for which in range(2):
        for batch in batches(chans):
            series = [
                jnp.concatenate(
                    [
                        filters[which, channel_rows(group), t * LANES : (t + 1) * LANES]
                        for t in range(blocks)
                    ],
                    axis=0,
                )
                for group in batch
            ]
            for group, spectrum in zip(batch, forward(series, tables)):
                spectra[which, group] = spectrum


def halves(array):
    lane = lax.broadcasted_iota(jnp.int32, array.shape, 1)
    return pltpu.roll(array, LANES // 2, 1), lane < LANES // 2


def packed_parts(rows):
    half = rows // 2
    marks = [0, rows, rows + half, 2 * rows + half, 2 * rows + half + 8]
    return [slice(low, high) for low, high in zip(marks[:-1], marks[1:])]


def pack_kernel(token_ids, w_in_far, cotangent_far, packed_far, w_in, cotangent, packed, sems):
    peers = packed.shape[0]
    rows, wide = w_in.shape
    half = rows // 2
    part_two, part_one, part_time, part_ids = packed_parts(rows)
    arrivals = [
        pltpu.make_async_copy(far, near, sems.at[place])
        for place, (far, near) in enumerate(((w_in_far, w_in), (cotangent_far, cotangent)))
    ]
    for copy in arrivals:
        copy.start()
    ids = widen(token_ids[...]).astype(BF16)
    for copy in arrivals:
        copy.wait()
    departures = []
    for pair in range(peers // 2):
        tiles = []
        for column in range(3):
            start = column * (wide // 3) + pair * LANES
            tile = widen(w_in[:, start : start + LANES])
            turned, first = halves(tile)
            tiles.append((tile, turned))
        first_half = first[:half]
        (zero, zero_turned), (one, one_turned), (two, two_turned) = tiles
        even, odd = 2 * pair, 2 * pair + 1
        packed[even, part_two, :] = jnp.where(first, zero, one_turned).astype(BF16)
        packed[odd, part_two, :] = jnp.where(first, zero_turned, one).astype(BF16)
        packed[even, part_one, :] = jnp.where(first_half, two[:half], two_turned[half:]).astype(
            BF16
        )
        packed[odd, part_one, :] = jnp.where(first_half, two_turned[:half], two[half:]).astype(
            BF16
        )
        turned = widen(cotangent[:, pair * LANES : (pair + 1) * LANES]).T.astype(BF16)
        packed[even, part_time, :] = turned[:rows]
        packed[odd, part_time, :] = turned[rows:]
        packed[even, part_ids, :] = ids
        packed[odd, part_ids, :] = ids
        both = pl.ds(even, 2)
        departures.append(
            pltpu.make_async_copy(packed.at[both], packed_far.at[both], sems.at[2 + pair])
        )
        departures[-1].start()
    for copy in departures:
        copy.wait()


def unpack_kernel(packed, mixer_out, weight_grads, tap_grads):
    peers = packed.shape[0]
    rows, wide = weight_grads.shape
    half = rows // 2
    part_two, part_one, part_time, part_taps = packed_parts(rows)
    for pair in range(peers // 2):
        even, odd = 2 * pair, 2 * pair + 1
        starts = [column * (wide // 3) + pair * LANES for column in range(3)]
        lanes = [slice(start, start + LANES) for start in starts]

        def merged(low, high):
            low_turned, first = halves(low)
            high_turned, _ = halves(high)
            return jnp.where(first, low, high_turned), jnp.where(first, low_turned, high)

        zero, one = merged(widen(packed[even, part_two, :]), widen(packed[odd, part_two, :]))
        weight_grads[:, lanes[0]] = zero
        weight_grads[:, lanes[1]] = one
        upper, lower = merged(widen(packed[even, part_one, :]), widen(packed[odd, part_one, :]))
        weight_grads[:half, lanes[2]] = upper
        weight_grads[half:, lanes[2]] = lower
        both = widen(jnp.concatenate([packed[even, part_time, :], packed[odd, part_time, :]], 0))
        mixer_out[:, pair * LANES : (pair + 1) * LANES] = both.T.astype(BF16)
        low = widen(packed[even, part_taps, :])
        high = widen(packed[odd, part_taps, :])
        zero, one = merged(low, high)
        tap_grads[:, lanes[0]] = zero[:3]
        tap_grads[:, lanes[1]] = one[:3]
        tap_grads[:, lanes[2]] = zero[3:6]


def mixer_kernel(packed_form, *refs):
    if packed_form:
        arrived_far, refs = refs[0], refs[1:]
        arrived, refs = refs[-1], refs[:-1]
        chans = refs[0].shape[0] // arrived.shape[0]
        part_two, part_one, part_time, part_small = packed_parts(chans)
        width = refs[0].shape[1]
        cotangent = arrived.at[:, part_time, :]

        def ids_of(block):
            return arrived[block, part_small, :]

    else:
        w_cols, ids, cotangent = refs[0][...], refs[1], refs[2]
        refs = refs[3:]
        chans = cotangent.shape[1]

        def ids_of(block):
            return ids[block]

    far, refs = refs[:9], refs[9:]
    lagged_far, refs = refs[0], refs[1:]
    if packed_form:
        sent_far, refs = refs[0], refs[1:]
    else:
        (mixer_out, weight_part, tap_terms), refs = refs[:3], refs[3:]
    near, refs = refs[:9], refs[9:]
    sems, lagged_spec, hot, proj, mixed, grad_mixed, grad_proj = refs[:7]
    if packed_form:
        sent = refs[7]
        mixer_out = sent.at[:, part_time, :]
    entries, taps, filter_spec = near[:3]
    tables = near[3:]
    blocks = mixed.shape[0]
    codes = LANES
    arrivals = [
        pltpu.make_async_copy(source, target, sems.at[place])
        for place, (source, target) in enumerate(zip(far[1:], near[1:]))
    ]
    quarter = entries.shape[0] // QUARTERS
    quarters = [slice(part * quarter, (part + 1) * quarter) for part in range(QUARTERS)]
    entry_arrivals = [
        pltpu.make_async_copy(far[0].at[rows], entries.at[rows], sems.at[len(arrivals) + part])
        for part, rows in enumerate(quarters)
    ]
    taken = len(arrivals) + QUARTERS
    if packed_form:
        first = pltpu.make_async_copy(arrived_far, arrived, sems.at[taken])
        first.start()
    for copy in entry_arrivals:
        copy.start()
    if packed_form:
        first.wait()
    for copy in arrivals:
        copy.start()
    departures = []

    def depart(source, target):
        departures.append(
            pltpu.make_async_copy(source, target, sems.at[taken + 1 + len(departures)])
        )
        departures[-1].start()

    for block in range(blocks):
        hot[:, block * LANES : (block + 1) * LANES] = one_hot(ids_of(block), codes)
    if packed_form:
        two = widen(flat(arrived[:, part_two, :]))
        one = widen(arrived[:, part_one, :])
        one_turned = pltpu.roll(flat(one), LANES // 2, 1).reshape(one.shape)
        one = flat(jnp.concatenate([one, one_turned], axis=1))
        w_cols = jnp.concatenate([two, one], axis=1).astype(BF16)
    coded = []
    for copy, rows in zip(entry_arrivals, quarters):
        copy.wait()
        coded.append(dot(entries[rows], w_cols).T[: 3 * chans].astype(BF16))
    coded = jnp.concatenate(coded, axis=1)
    arrivals[0].wait()
    lane = lax.broadcasted_iota(jnp.int32, (3 * chans, LANES), 1)
    last1 = jnp.zeros((3 * chans, LANES), F32)
    last2 = last1
    for pair in range(blocks // 2):
        lanes = slice(2 * pair * LANES, (2 * pair + 2) * LANES)
        both = dot(coded, hot[:, lanes]).astype(BF16)
        for side in range(2):
            block = 2 * pair + side
            now = both[:, side * LANES : (side + 1) * LANES]
            proj[block] = now
            now = widen(now)
            turn1 = pltpu.roll(now, 1, 1)
            turn2 = pltpu.roll(now, 2, 1)
            late1 = jnp.where(lane < 1, last1, turn1)
            late2 = jnp.where(lane < 2, last2, turn2)
            last1, last2 = turn1, turn2
            mixed[block] = (taps[0] * now + taps[1] * late1 + taps[2] * late2).astype(BF16)

    def column(ref, group, place=0):
        return flat(ref[:, channel_rows(group, place * chans), :])

    def blocked(value):
        return value.reshape(blocks, GROUP, LANES)

    for copy in arrivals[1:]:
        copy.wait()
    for batch in batches(chans):
        value_spec = forward([column(mixed, group) for group in batch], tables)
        turned = [
            product(spectrum, filter_spec[0, group], False)
            for group, spectrum in zip(batch, value_spec)
        ]
        first_conv = [rounded(signal) for signal in inverse(turned, tables)]
        series = [
            (widen(column(mixed, group, 1)) * conv).astype(BF16)
            for group, conv in zip(batch, first_conv)
        ]
        mix_spec = forward(series, tables)
        turned = [
            product(spectrum, filter_spec[1, group], False)
            for group, spectrum in zip(batch, mix_spec)
        ]
        series = []
        for group, signal in zip(batch, inverse(turned, tables)):
            second_conv = rounded(signal)
            gate = widen(column(mixed, group, 2))
            upstream = widen(column(cotangent, group))
            mixer_out[:, channel_rows(group), :] = blocked((gate * second_conv).astype(BF16))
            grad_mixed[:, channel_rows(group, 2 * chans), :] = blocked(
                (upstream * second_conv).astype(BF16)
            )
            series.append((upstream * gate).astype(BF16))
        grad_spec = forward(series, tables)
        turned = []
        for place, group in enumerate(batch):
            lagged_spec[1, group] = product(grad_spec[place], mix_spec[place], True).astype(BF16)
            turned.append(product(grad_spec[place], filter_spec[1, group], True))
        series = []
        for place, signal in enumerate(inverse(turned, tables)):
            grad_mix = rounded(signal)
            group = batch[place]
            grad_mixed[:, channel_rows(group, chans), :] = blocked(
                (grad_mix * first_conv[place]).astype(BF16)
            )
            series.append((grad_mix * widen(column(mixed, group, 1))).astype(BF16))
        grad_spec = forward(series, tables)
        turned = []
        for place, group in enumerate(batch):
            lagged_spec[0, group] = product(grad_spec[place], value_spec[place], True).astype(BF16)
            turned.append(product(grad_spec[place], filter_spec[0, group], True))
        some = pl.ds(batch[0], len(batch))
        depart(lagged_spec.at[:, some], lagged_far.at[:, some])
        for group, signal in zip(batch, inverse(turned, tables)):
            grad_mixed[:, channel_rows(group), :] = blocked(signal.astype(BF16))

    next1 = jnp.zeros((3 * chans, LANES), F32)
    next2 = next1
    sums = [next1] * 3
    for block in reversed(range(blocks)):
        now = widen(grad_mixed[block])
        turn1 = pltpu.roll(now, LANES - 1, 1)
        turn2 = pltpu.roll(now, LANES - 2, 1)
        soon1 = jnp.where(lane >= LANES - 1, next1, turn1)
        soon2 = jnp.where(lane >= LANES - 2, next2, turn2)
        next1, next2 = turn1, turn2
        grad_proj[:, block * LANES : (block + 1) * LANES] = (
            taps[0] * now + taps[1] * soon1 + taps[2] * soon2
        ).astype(BF16)
        held = widen(proj[block])
        sums = [total + held * moved for total, moved in zip(sums, (now, soon1, soon2))]
    coded = lax.dot_general(
        grad_proj[...], hot[...], (((1,), (1,)), ((), ())), preferred_element_type=F32
    )
    coded = coded.astype(BF16)
    if not packed_form:
        weights = dot(coded, entries[...])
        weight_part[...] = weights.T.astype(BF16)
        for tap in range(3):
            tap_terms[tap] = jnp.sum(sums[tap], axis=1, keepdims=True)
        for copy in departures:
            copy.wait()
        return
    for tap in range(3):
        sums[tap] = jnp.sum(sums[tap].T, axis=0, keepdims=True)
    space = jnp.zeros((1, LANES), F32)
    total = jnp.concatenate(
        [sums[tap][:, :LANES] for tap in range(3)]
        + [
            jnp.concatenate([sums[tap][:, LANES:], space[:, : LANES - chans]], axis=1)
            for tap in range(3)
        ]
        + [space] * 2,
        axis=0,
    )
    for block in range(blocks):
        sent[block, part_small, :] = total.astype(BF16)
    half = chans // 2
    for columns in quarters:
        weights = dot(coded, entries[:, columns])
        some = slice(columns.start // chans, columns.stop // chans)
        two = weights[: 2 * chans].T
        sent[some, part_two, :] = two.astype(BF16).reshape(-1, chans, LANES)
        space = jnp.zeros((LANES - chans, weights.shape[1]), F32)
        one = jnp.concatenate([weights[2 * chans :], space], axis=0).T
        one = one.reshape(-1, chans, LANES)
        turned = pltpu.roll(flat(one[:, half:]), LANES // 2, 1)
        one = flat(one[:, :half])
        lane = lax.broadcasted_iota(jnp.int32, one.shape, 1)
        one = jnp.where(lane < LANES // 2, one, turned)
        sent[some, part_one, :] = one.astype(BF16).reshape(-1, half, LANES)
        depart(sent.at[some], sent_far.at[some])
    for copy in departures:
        copy.wait()


def lagged_kernel(lagged_spec, *rest):
    tables, filter_grads = rest[:6], rest[6]
    chans, steps = filter_grads.shape[1:]
    blocks = steps // LANES
    for which in range(2):
        for batch in batches(chans):
            turned = [lagged_spec[which, group] for group in batch]
            for group, signal in zip(batch, inverse(turned, tables)):
                for t in range(blocks):
                    filter_grads[which, channel_rows(group), t * LANES : (t + 1) * LANES] = signal[
                        t * GROUP : (t + 1) * GROUP
                    ]


def shape(dims, kind):
    return jax.ShapeDtypeStruct(dims, kind)


def exchange(blocks):
    return lax.all_to_all(blocks, "tm", split_axis=0, concat_axis=0, tiled=True)


def call(kernel, name, megabytes, **settings):
    return pl.pallas_call(
        kernel,
        name=name,
        compiler_params=pltpu.CompilerParams(vmem_limit_bytes=int(megabytes * 1024 * 1024)),
        **settings,
    )


def send_inputs(token_ids, w_in, cotangent, peers):
    tok_rows, width = cotangent.shape
    rows, fields, chans = w_in.shape[0], token_ids.shape[1], width // peers
    w_send = w_in.reshape(rows, 3, peers, chans).transpose(2, 0, 1, 3)
    w_send = w_send.reshape(peers, rows * 3 * chans // LANES, LANES)
    ids_send = jnp.broadcast_to(token_ids.T.astype(BF16)[None], (peers, fields, tok_rows))
    cot_send = cotangent.T.reshape(peers, chans, tok_rows)
    arrived = exchange(jnp.concatenate([w_send, ids_send, cot_send], axis=1))
    count = w_send.shape[1]
    w_cols = arrived[:, :count].reshape(width, 3 * chans)
    return w_cols, arrived[:, count : count + fields], arrived[:, count + fields :]


def send_results(mixer_out, weight_part, tap_terms, peers, rows):
    _, chans, tok_rows = mixer_out.shape
    width = peers * chans
    count = 9 * chans
    tap_terms = tap_terms.reshape(1, count)
    tap_high = tap_terms.astype(BF16)
    tap_low = (tap_terms - widen(tap_high)).astype(BF16)
    tap_send = jnp.concatenate([tap_high, tap_low], axis=1)
    tap_send = jnp.pad(tap_send, ((0, 0), (0, -2 * count % LANES))).reshape(1, -1, LANES)
    tap_send = jnp.broadcast_to(tap_send, (peers,) + tap_send.shape[1:])
    weight_send = weight_part.reshape(peers, rows * 3 * chans // LANES, LANES)
    arrived = exchange(jnp.concatenate([mixer_out, weight_send, tap_send], axis=1))
    mixer_out = arrived[:, :chans].reshape(width, tok_rows).T
    place = chans + weight_send.shape[1]
    weight_grads = arrived[:, chans:place].reshape(peers, rows, 3, chans)
    weight_grads = widen(weight_grads).transpose(1, 2, 0, 3).reshape(rows, 3 * width)
    taps_moved = arrived[:, place:].reshape(peers, -1)
    tap_grads = widen(taps_moved[:, :count]) + widen(taps_moved[:, count : 2 * count])
    tap_grads = tap_grads.reshape(peers, 3, 3, chans).transpose(1, 2, 0, 3)
    return mixer_out, weight_grads, tap_grads.reshape(3, 3 * width)


def local(token_ids, field_offsets, embed_table, w_in, short_taps, filters, cotangent):
    tok_rows, width = cotangent.shape
    peers = lax.axis_size("tm")
    fields = token_ids.shape[1]
    rows = w_in.shape[0]
    chans = width // peers
    steps = tok_rows * peers
    groups = chans // GROUP
    tables = transform_tables(peers)
    packed_form = 2 * chans == LANES and rows == chans and fields == 8
    spec = (2, groups, peers * GROUP, 2 * LANES)
    moved = (peers, chans, LANES)
    wide = (peers, 3 * chans, LANES)
    packed = shape((peers, packed_parts(rows)[-1].stop, LANES), BF16)

    near = pl.BlockSpec(memory_space=pltpu.VMEM)
    far = pl.BlockSpec(memory_space=pltpu.HBM)

    if packed_form:
        sent = call(
            pack_kernel,
            "pack",
            PACK_MB,
            in_specs=[near, far, far],
            out_specs=far,
            out_shape=packed,
            scratch_shapes=[
                pltpu.VMEM(w_in.shape, BF16),
                pltpu.VMEM(cotangent.shape, BF16),
                pltpu.VMEM(packed.shape, BF16),
                pltpu.SemaphoreType.DMA((2 + peers // 2,)),
            ],
        )(token_ids.T, w_in, cotangent)
        arrived = (exchange(sent),)
    else:
        arrived = send_inputs(token_ids, w_in, cotangent, peers)

    taps = short_taps.reshape(3, 3, peers, chans)
    taps = lax.dynamic_index_in_dim(taps, lax.axis_index("tm"), axis=2, keepdims=False)
    filter_spec, entries, taps = call(
        prepare_kernel,
        "prepare",
        32,
        in_specs=[pl.BlockSpec(memory_space=pltpu.SMEM)] + [near] * 9,
        out_shape=(
            shape(spec, F32),
            shape(embed_table.shape, BF16),
            shape((3, 3 * chans, LANES), F32),
        ),
        cost_estimate=pl.CostEstimate(
            flops=10**10, bytes_accessed=3 * 10**7, transcendentals=0
        ),
    )(field_offsets, filters, embed_table, taps.reshape(3, 3 * chans, 1), *tables)
    if packed_form:
        out_shape = (shape(spec, BF16), packed)
        out_specs = (far, far)
        scratch_shapes = [pltpu.VMEM(packed.shape, BF16)] * 2
    else:
        out_shape = (
            shape(spec, BF16),
            shape(moved, BF16),
            shape((width, 3 * chans), BF16),
            shape((3, 3 * chans, 1), F32),
        )
        out_specs = (far, near, near, near)
        scratch_shapes = []
    operands = (entries, taps, filter_spec) + tables
    results = call(
        functools.partial(mixer_kernel, packed_form),
        "mixer",
        MIX_MB,
        in_specs=[far if packed_form else near] * len(arrived) + [far] * len(operands),
        out_shape=out_shape,
        out_specs=out_specs,
        scratch_shapes=[pltpu.VMEM(operand.shape, operand.dtype) for operand in operands]
        + [
            pltpu.SemaphoreType.DMA((len(operands) + groups + 2 * QUARTERS,)),
            pltpu.VMEM(spec, BF16),
            pltpu.VMEM((embed_table.shape[0], steps), BF16),
            pltpu.VMEM(wide, BF16),
            pltpu.VMEM(wide, BF16),
            pltpu.VMEM(wide, BF16),
            pltpu.VMEM((3 * chans, steps), BF16),
        ]
        + scratch_shapes,
    )(*arrived, *operands)
    filter_grads = call(
        lagged_kernel,
        "lagged",
        24,
        out_shape=shape((2, chans, steps), F32),
        cost_estimate=pl.CostEstimate(
            flops=10**10, bytes_accessed=3 * 10**7, transcendentals=0
        ),
    )(results[0], *tables)
    if packed_form:
        mixer_out, weight_grads, tap_grads = call(
            unpack_kernel,
            "unpack",
            16,
            out_shape=(
                shape((tok_rows, width), BF16),
                shape((rows, 3 * width), F32),
                shape((3, 3 * width), F32),
            ),
        )(exchange(results[1]))
    else:
        mixer_out, weight_grads, tap_grads = send_results(*results[1:], peers, rows)
    return (mixer_out, weight_grads, tap_grads, filter_grads)


def solution(mesh):
    return jax.shard_map(
        local,
        mesh=mesh,
        in_specs=(
            P(("groups", "tm"), None),
            P("groups"),
            P(),
            P("tm", None),
            P(),
            P(None, "tm", None),
            P(("groups", "tm"), None),
        ),
        out_specs=(
            P(("groups", "tm"), None),
            P(("groups", "tm"), None),
            P("groups", None),
            P("groups", "tm", None),
        ),
        check_vma=False,
    )
```

```python
import functools
import math


import jax
import jax.numpy as jnp
import ml_dtypes
import numpy as np
from jax import lax
from jax.experimental import pallas as pl
from jax.experimental.pallas import tpu as pltpu
from jax.sharding import PartitionSpec as P

F32 = jnp.float32
BF16 = jnp.bfloat16
LANES = 128
GROUP = 16
QUARTERS = 2
PACK_MB = 62
MIX_MB = 61.5


def widen(array):
    return array.astype(F32)


def rounded(array):
    return array.astype(BF16).astype(F32)


def transform_tables(blocks):
    total = 2 * blocks * LANES
    row = np.arange(blocks) + 0.5
    first = np.exp(-2j * np.pi * np.outer(row, np.arange(blocks)) / (2 * blocks))
    turn = np.exp(-2j * np.pi * np.outer(row, np.arange(LANES)) / total)
    second = np.exp(-2j * np.pi * np.outer(np.arange(LANES), np.arange(LANES)) / LANES)
    same = np.eye(GROUP)
    first_rows = np.concatenate([first.real, first.imag], axis=0)
    back_rows = np.concatenate([first.real.T, first.imag.T], axis=1) * (2.0 / total)
    forward = np.block([[second.real, second.imag], [-second.imag, second.real]])
    inverse = np.block([[second.real, -second.imag], [second.imag, second.real]])
    narrow = ml_dtypes.bfloat16
    return (
        np.kron(first_rows, same).astype(narrow),
        np.kron(back_rows, same).astype(narrow),
        forward.astype(narrow),
        inverse.astype(narrow),
        np.repeat(turn.real, GROUP, axis=0).astype(np.float32),
        np.repeat(turn.imag, GROUP, axis=0).astype(np.float32),
    )


def dot(left, right):
    return jnp.dot(left, right, preferred_element_type=F32)


def joined(parts, axis):
    return parts[0] if len(parts) == 1 else jnp.concatenate(parts, axis=axis)


def forward(series, tables):
    first, _, second, _, turn_re, turn_im = tables
    rows = turn_re.shape[0]
    part = dot(first[...], joined(series, 1))
    spectra = []
    for place in range(len(series)):
        lanes = slice(place * LANES, (place + 1) * LANES)
        part_re = part[:rows, lanes]
        part_im = part[rows:, lanes]
        turned = jnp.concatenate(
            [
                part_re * turn_re[...] - part_im * turn_im[...],
                part_re * turn_im[...] + part_im * turn_re[...],
            ],
            axis=1,
        )
        spectra.append(dot(turned.astype(BF16), second[...]))
    return spectra


def inverse(spectra, tables):
    _, last, _, second, turn_re, turn_im = tables
    turned = []
    for spectrum in spectra:
        back = dot(spectrum.astype(BF16), second[...])
        back_re = back[:, :LANES]
        back_im = back[:, LANES:]
        turned.append(
            jnp.concatenate(
                [
                    back_re * turn_re[...] + back_im * turn_im[...],
                    back_im * turn_re[...] - back_re * turn_im[...],
                ],
                axis=0,
            ).astype(BF16)
        )
    signal = dot(last[...], joined(turned, 1))
    return [signal[:, place * LANES : (place + 1) * LANES] for place in range(len(spectra))]


def product(left, right, conjugate):
    left_re, left_im = left[:, :LANES], left[:, LANES:]
    right_re, right_im = right[:, :LANES], right[:, LANES:]
    if conjugate:
        return jnp.concatenate(
            [
                left_re * right_re + left_im * right_im,
                left_im * right_re - left_re * right_im,
            ],
            axis=1,
        )
    return jnp.concatenate(
        [
            left_re * right_re - left_im * right_im,
            left_re * right_im + left_im * right_re,
        ],
        axis=1,
    )


def batches(chans):
    groups = chans // GROUP
    size = math.gcd(groups, 4)
    return [range(start, start + size) for start in range(0, groups, size)]


def channel_rows(group, offset=0):
    return slice(offset + group * GROUP, offset + (group + 1) * GROUP)


def flat(block):
    return block.reshape(block.shape[0] * block.shape[1], block.shape[2])


def one_hot(ids, codes):
    fields, lanes = ids.shape
    code = lax.broadcasted_iota(jnp.int32, (codes, lanes), 0).astype(F32).astype(BF16)
    one, zero = jnp.ones((codes, lanes), BF16), jnp.zeros((codes, lanes), BF16)
    return jnp.concatenate(
        [jnp.where(code == ids[field : field + 1], one, zero) for field in range(fields)],
        axis=0,
    )


def narrow_places(tables):
    places, low = [], 0
    for which in range(4):
        rows, columns = tables[which].shape
        for start in range(0, columns, 2 * LANES):
            places.append((low, low + rows, which, slice(start, start + 2 * LANES)))
            low += rows
    return places


def prepare_kernel(offsets, filters, table, short_taps, *rest):
    tables = rest[:6]
    spectra, entries, narrow, wide = rest[6:]
    for low, high, which, lanes in narrow_places(tables):
        narrow[low:high] = tables[which][:, lanes]
    count = short_taps.shape[1]
    rows = tables[4].shape[0]
    for tap in range(3):
        wide[tap * count : (tap + 1) * count] = jnp.broadcast_to(short_taps[tap], (count, LANES))
    for part in range(2):
        start = 3 * count + part * rows
        wide[start : start + rows] = tables[4 + part][...]
    chans, steps = filters.shape[1:]
    blocks = steps // LANES
    fields = offsets.shape[0]
    codes = entries.shape[0] // fields
    window = codes + GROUP
    for field in range(fields):
        start = jnp.minimum(offsets[field] // GROUP * GROUP, table.shape[0] - window)
        row = lax.broadcasted_iota(jnp.int32, (codes, window), 0) + (offsets[field] - start)
        place = lax.broadcasted_iota(jnp.int32, (codes, window), 1)
        picked = jnp.where(row == place, 1.0, 0.0).astype(BF16)
        entries[field * codes : (field + 1) * codes, :] = dot(
            picked, table[pl.ds(pl.multiple_of(start, GROUP), window), :]
        ).astype(BF16)
    for which in range(2):
        for batch in batches(chans):
            series = [
                jnp.concatenate(
                    [
                        filters[which, channel_rows(group), t * LANES : (t + 1) * LANES]
                        for t in range(blocks)
                    ],
                    axis=0,
                )
                for group in batch
            ]
            for group, spectrum in zip(batch, forward(series, tables)):
                spectra[which, group] = spectrum


def halves(array):
    lane = lax.broadcasted_iota(jnp.int32, array.shape, 1)
    return pltpu.roll(array, LANES // 2, 1), lane < LANES // 2


def packed_parts(rows):
    half = rows // 2
    marks = [0, rows, rows + half, 2 * rows + half, 2 * rows + half + 8]
    return [slice(low, high) for low, high in zip(marks[:-1], marks[1:])]


def pack_kernel(token_ids, w_in_far, cotangent_far, packed_far, w_in, cotangent, packed, sems):
    peers = packed.shape[0]
    rows, wide = w_in.shape
    half = rows // 2
    part_two, part_one, part_time, part_ids = packed_parts(rows)
    arrivals = [
        pltpu.make_async_copy(far, near, sems.at[place])
        for place, (far, near) in enumerate(((w_in_far, w_in), (cotangent_far, cotangent)))
    ]
    for copy in arrivals:
        copy.start()
    ids = widen(token_ids[...]).astype(BF16)
    for copy in arrivals:
        copy.wait()
    departures = []
    for pair in range(peers // 2):
        tiles = []
        for column in range(3):
            start = column * (wide // 3) + pair * LANES
            tile = widen(w_in[:, start : start + LANES])
            turned, first = halves(tile)
            tiles.append((tile, turned))
        first_half = first[:half]
        (zero, zero_turned), (one, one_turned), (two, two_turned) = tiles
        even, odd = 2 * pair, 2 * pair + 1
        packed[even, part_two, :] = jnp.where(first, zero, one_turned).astype(BF16)
        packed[odd, part_two, :] = jnp.where(first, zero_turned, one).astype(BF16)
        packed[even, part_one, :] = jnp.where(first_half, two[:half], two_turned[half:]).astype(
            BF16
        )
        packed[odd, part_one, :] = jnp.where(first_half, two_turned[:half], two[half:]).astype(
            BF16
        )
        turned = widen(cotangent[:, pair * LANES : (pair + 1) * LANES]).T.astype(BF16)
        packed[even, part_time, :] = turned[:rows]
        packed[odd, part_time, :] = turned[rows:]
        packed[even, part_ids, :] = ids
        packed[odd, part_ids, :] = ids
        both = pl.ds(even, 2)
        departures.append(
            pltpu.make_async_copy(packed.at[both], packed_far.at[both], sems.at[2 + pair])
        )
        departures[-1].start()
    for copy in departures:
        copy.wait()


def unpack_kernel(packed, mixer_out, weight_grads, tap_grads):
    peers = packed.shape[0]
    rows, wide = weight_grads.shape
    half = rows // 2
    part_two, part_one, part_time, part_taps = packed_parts(rows)
    for pair in range(peers // 2):
        even, odd = 2 * pair, 2 * pair + 1
        starts = [column * (wide // 3) + pair * LANES for column in range(3)]
        lanes = [slice(start, start + LANES) for start in starts]

        def merged(low, high):
            low_turned, first = halves(low)
            high_turned, _ = halves(high)
            return jnp.where(first, low, high_turned), jnp.where(first, low_turned, high)

        zero, one = merged(widen(packed[even, part_two, :]), widen(packed[odd, part_two, :]))
        weight_grads[:, lanes[0]] = zero
        weight_grads[:, lanes[1]] = one
        upper, lower = merged(widen(packed[even, part_one, :]), widen(packed[odd, part_one, :]))
        weight_grads[:half, lanes[2]] = upper
        weight_grads[half:, lanes[2]] = lower
        both = widen(jnp.concatenate([packed[even, part_time, :], packed[odd, part_time, :]], 0))
        mixer_out[:, pair * LANES : (pair + 1) * LANES] = both.T.astype(BF16)
        low = widen(packed[even, part_taps, :])
        high = widen(packed[odd, part_taps, :])
        zero, one = merged(low, high)
        tap_grads[:, lanes[0]] = zero[:3]
        tap_grads[:, lanes[1]] = one[:3]
        tap_grads[:, lanes[2]] = zero[3:6]


def mixer_kernel(packed_form, *refs):
    if packed_form:
        arrived_far, refs = refs[0], refs[1:]
        arrived, refs = refs[-1], refs[:-1]
        chans = refs[0].shape[0] // arrived.shape[0]
        part_two, part_one, part_time, part_small = packed_parts(chans)
        width = refs[0].shape[1]
        cotangent = arrived.at[:, part_time, :]

        def ids_of(block):
            return arrived[block, part_small, :]

    else:
        w_cols, ids, cotangent = refs[0][...], refs[1], refs[2]
        refs = refs[3:]
        chans = cotangent.shape[1]

        def ids_of(block):
            return ids[block]

    (entries_far, filter_far, narrow_far, wide_far), refs = refs[:4], refs[4:]
    lagged_far, refs = refs[0], refs[1:]
    if packed_form:
        sent_far, refs = refs[0], refs[1:]
    else:
        (mixer_out, weight_part, tap_terms), refs = refs[:3], refs[3:]
    near, refs = refs[:9], refs[9:]
    sems, lagged_spec, hot, proj, mixed, grad_mixed, grad_proj = refs[:7]
    if packed_form:
        sent = refs[7]
        mixer_out = sent.at[:, part_time, :]
    entries, taps, filter_spec = near[:3]
    tables = near[3:]
    blocks = mixed.shape[0]
    codes = LANES
    count = taps.shape[1]
    rows = tables[4].shape[0]
    parts = [(wide_far.at[pl.ds(tap * count, count)], taps.at[tap]) for tap in range(3)]
    parts.append((filter_far, filter_spec))
    for low, high, which, lanes in narrow_places(tables):
        lanes = pl.ds(lanes.start, 2 * LANES)
        parts.append((narrow_far.at[pl.ds(low, high - low)], tables[which].at[:, lanes]))
    for part in range(2):
        parts.append((wide_far.at[pl.ds(3 * count + part * rows, rows)], tables[4 + part]))
    arrivals = [
        pltpu.make_async_copy(source, target, sems.at[place])
        for place, (source, target) in enumerate(parts)
    ]
    quarter = entries.shape[0] // QUARTERS
    quarters = [slice(part * quarter, (part + 1) * quarter) for part in range(QUARTERS)]
    entry_arrivals = [
        pltpu.make_async_copy(entries_far.at[rows], entries.at[rows], sems.at[len(arrivals) + part])
        for part, rows in enumerate(quarters)
    ]
    taken = len(arrivals) + QUARTERS
    if packed_form:
        first = pltpu.make_async_copy(arrived_far, arrived, sems.at[taken])
        first.start()
    for copy in entry_arrivals:
        copy.start()
    if packed_form:
        first.wait()
    for copy in arrivals:
        copy.start()
    departures = []

    def depart(source, target):
        departures.append(
            pltpu.make_async_copy(source, target, sems.at[taken + 1 + len(departures)])
        )
        departures[-1].start()

    for block in range(blocks):
        hot[:, block * LANES : (block + 1) * LANES] = one_hot(ids_of(block), codes)
    if packed_form:
        two = widen(flat(arrived[:, part_two, :]))
        one = widen(arrived[:, part_one, :])
        one_turned = pltpu.roll(flat(one), LANES // 2, 1).reshape(one.shape)
        one = flat(jnp.concatenate([one, one_turned], axis=1))
        w_cols = jnp.concatenate([two, one], axis=1).astype(BF16)
    coded = []
    for copy, rows in zip(entry_arrivals, quarters):
        copy.wait()
        coded.append(dot(entries[rows], w_cols).T[: 3 * chans].astype(BF16))
    coded = jnp.concatenate(coded, axis=1)
    for copy in arrivals[:3]:
        copy.wait()
    lane = lax.broadcasted_iota(jnp.int32, (3 * chans, LANES), 1)
    last1 = jnp.zeros((3 * chans, LANES), F32)
    last2 = last1
    for pair in range(blocks // 2):
        lanes = slice(2 * pair * LANES, (2 * pair + 2) * LANES)
        both = dot(coded, hot[:, lanes]).astype(BF16)
        for side in range(2):
            block = 2 * pair + side
            now = both[:, side * LANES : (side + 1) * LANES]
            proj[block] = now
            now = widen(now)
            turn1 = pltpu.roll(now, 1, 1)
            turn2 = pltpu.roll(now, 2, 1)
            late1 = jnp.where(lane < 1, last1, turn1)
            late2 = jnp.where(lane < 2, last2, turn2)
            last1, last2 = turn1, turn2
            mixed[block] = (taps[0] * now + taps[1] * late1 + taps[2] * late2).astype(BF16)

    def column(ref, group, place=0):
        return flat(ref[:, channel_rows(group, place * chans), :])

    def blocked(value):
        return value.reshape(blocks, GROUP, LANES)

    for copy in arrivals[3:]:
        copy.wait()
    for batch in batches(chans):
        value_spec = forward([column(mixed, group) for group in batch], tables)
        turned = [
            product(spectrum, filter_spec[0, group], False)
            for group, spectrum in zip(batch, value_spec)
        ]
        first_conv = [rounded(signal) for signal in inverse(turned, tables)]
        series = [
            (widen(column(mixed, group, 1)) * conv).astype(BF16)
            for group, conv in zip(batch, first_conv)
        ]
        mix_spec = forward(series, tables)
        turned = [
            product(spectrum, filter_spec[1, group], False)
            for group, spectrum in zip(batch, mix_spec)
        ]
        series = []
        for group, signal in zip(batch, inverse(turned, tables)):
            second_conv = rounded(signal)
            gate = widen(column(mixed, group, 2))
            upstream = widen(column(cotangent, group))
            mixer_out[:, channel_rows(group), :] = blocked((gate * second_conv).astype(BF16))
            grad_mixed[:, channel_rows(group, 2 * chans), :] = blocked(
                (upstream * second_conv).astype(BF16)
            )
            series.append((upstream * gate).astype(BF16))
        grad_spec = forward(series, tables)
        turned = []
        for place, group in enumerate(batch):
            lagged_spec[1, group] = product(grad_spec[place], mix_spec[place], True).astype(BF16)
            turned.append(product(grad_spec[place], filter_spec[1, group], True))
        series = []
        for place, signal in enumerate(inverse(turned, tables)):
            grad_mix = rounded(signal)
            group = batch[place]
            grad_mixed[:, channel_rows(group, chans), :] = blocked(
                (grad_mix * first_conv[place]).astype(BF16)
            )
            series.append((grad_mix * widen(column(mixed, group, 1))).astype(BF16))
        grad_spec = forward(series, tables)
        turned = []
        for place, group in enumerate(batch):
            lagged_spec[0, group] = product(grad_spec[place], value_spec[place], True).astype(BF16)
            turned.append(product(grad_spec[place], filter_spec[0, group], True))
        some = pl.ds(batch[0], len(batch))
        depart(lagged_spec.at[:, some], lagged_far.at[:, some])
        for group, signal in zip(batch, inverse(turned, tables)):
            grad_mixed[:, channel_rows(group), :] = blocked(signal.astype(BF16))

    next1 = jnp.zeros((3 * chans, LANES), F32)
    next2 = next1
    sums = [next1] * 3
    for block in reversed(range(blocks)):
        now = widen(grad_mixed[block])
        turn1 = pltpu.roll(now, LANES - 1, 1)
        turn2 = pltpu.roll(now, LANES - 2, 1)
        soon1 = jnp.where(lane >= LANES - 1, next1, turn1)
        soon2 = jnp.where(lane >= LANES - 2, next2, turn2)
        next1, next2 = turn1, turn2
        grad_proj[:, block * LANES : (block + 1) * LANES] = (
            taps[0] * now + taps[1] * soon1 + taps[2] * soon2
        ).astype(BF16)
        held = widen(proj[block])
        sums = [total + held * moved for total, moved in zip(sums, (now, soon1, soon2))]
    coded = lax.dot_general(
        grad_proj[...], hot[...], (((1,), (1,)), ((), ())), preferred_element_type=F32
    )
    coded = coded.astype(BF16)
    if not packed_form:
        weights = dot(coded, entries[...])
        weight_part[...] = weights.T.astype(BF16)
        for tap in range(3):
            tap_terms[tap] = jnp.sum(sums[tap], axis=1, keepdims=True)
        for copy in departures:
            copy.wait()
        return
    for tap in range(3):
        sums[tap] = jnp.sum(sums[tap].T, axis=0, keepdims=True)
    space = jnp.zeros((1, LANES), F32)
    total = jnp.concatenate(
        [sums[tap][:, :LANES] for tap in range(3)]
        + [
            jnp.concatenate([sums[tap][:, LANES:], space[:, : LANES - chans]], axis=1)
            for tap in range(3)
        ]
        + [space] * 2,
        axis=0,
    )
    for block in range(blocks):
        sent[block, part_small, :] = total.astype(BF16)
    half = chans // 2
    for columns in quarters:
        weights = dot(coded, entries[:, columns])
        some = slice(columns.start // chans, columns.stop // chans)
        two = weights[: 2 * chans].T
        sent[some, part_two, :] = two.astype(BF16).reshape(-1, chans, LANES)
        space = jnp.zeros((LANES - chans, weights.shape[1]), F32)
        one = jnp.concatenate([weights[2 * chans :], space], axis=0).T
        one = one.reshape(-1, chans, LANES)
        turned = pltpu.roll(flat(one[:, half:]), LANES // 2, 1)
        one = flat(one[:, :half])
        lane = lax.broadcasted_iota(jnp.int32, one.shape, 1)
        one = jnp.where(lane < LANES // 2, one, turned)
        sent[some, part_one, :] = one.astype(BF16).reshape(-1, half, LANES)
        depart(sent.at[some], sent_far.at[some])
    for copy in departures:
        copy.wait()


def lagged_kernel(lagged_spec, *rest):
    tables, filter_grads = rest[:6], rest[6]
    chans, steps = filter_grads.shape[1:]
    blocks = steps // LANES
    for which in range(2):
        for batch in batches(chans):
            turned = [lagged_spec[which, group] for group in batch]
            for group, signal in zip(batch, inverse(turned, tables)):
                for t in range(blocks):
                    filter_grads[which, channel_rows(group), t * LANES : (t + 1) * LANES] = signal[
                        t * GROUP : (t + 1) * GROUP
                    ]


def shape(dims, kind):
    return jax.ShapeDtypeStruct(dims, kind)


def exchange(blocks):
    return lax.all_to_all(blocks, "tm", split_axis=0, concat_axis=0, tiled=True)


def call(kernel, name, megabytes, **settings):
    return pl.pallas_call(
        kernel,
        name=name,
        compiler_params=pltpu.CompilerParams(vmem_limit_bytes=int(megabytes * 1024 * 1024)),
        **settings,
    )


def send_inputs(token_ids, w_in, cotangent, peers):
    tok_rows, width = cotangent.shape
    rows, fields, chans = w_in.shape[0], token_ids.shape[1], width // peers
    w_send = w_in.reshape(rows, 3, peers, chans).transpose(2, 0, 1, 3)
    w_send = w_send.reshape(peers, rows * 3 * chans // LANES, LANES)
    ids_send = jnp.broadcast_to(token_ids.T.astype(BF16)[None], (peers, fields, tok_rows))
    cot_send = cotangent.T.reshape(peers, chans, tok_rows)
    arrived = exchange(jnp.concatenate([w_send, ids_send, cot_send], axis=1))
    count = w_send.shape[1]
    w_cols = arrived[:, :count].reshape(width, 3 * chans)
    return w_cols, arrived[:, count : count + fields], arrived[:, count + fields :]


def send_results(mixer_out, weight_part, tap_terms, peers, rows):
    _, chans, tok_rows = mixer_out.shape
    width = peers * chans
    count = 9 * chans
    tap_terms = tap_terms.reshape(1, count)
    tap_high = tap_terms.astype(BF16)
    tap_low = (tap_terms - widen(tap_high)).astype(BF16)
    tap_send = jnp.concatenate([tap_high, tap_low], axis=1)
    tap_send = jnp.pad(tap_send, ((0, 0), (0, -2 * count % LANES))).reshape(1, -1, LANES)
    tap_send = jnp.broadcast_to(tap_send, (peers,) + tap_send.shape[1:])
    weight_send = weight_part.reshape(peers, rows * 3 * chans // LANES, LANES)
    arrived = exchange(jnp.concatenate([mixer_out, weight_send, tap_send], axis=1))
    mixer_out = arrived[:, :chans].reshape(width, tok_rows).T
    place = chans + weight_send.shape[1]
    weight_grads = arrived[:, chans:place].reshape(peers, rows, 3, chans)
    weight_grads = widen(weight_grads).transpose(1, 2, 0, 3).reshape(rows, 3 * width)
    taps_moved = arrived[:, place:].reshape(peers, -1)
    tap_grads = widen(taps_moved[:, :count]) + widen(taps_moved[:, count : 2 * count])
    tap_grads = tap_grads.reshape(peers, 3, 3, chans).transpose(1, 2, 0, 3)
    return mixer_out, weight_grads, tap_grads.reshape(3, 3 * width)


def local(token_ids, field_offsets, embed_table, w_in, short_taps, filters, cotangent):
    tok_rows, width = cotangent.shape
    peers = lax.axis_size("tm")
    fields = token_ids.shape[1]
    rows = w_in.shape[0]
    chans = width // peers
    steps = tok_rows * peers
    groups = chans // GROUP
    tables = transform_tables(peers)
    packed_form = 2 * chans == LANES and rows == chans and fields == 8
    spec = (2, groups, peers * GROUP, 2 * LANES)
    moved = (peers, chans, LANES)
    wide = (peers, 3 * chans, LANES)
    packed = shape((peers, packed_parts(rows)[-1].stop, LANES), BF16)

    near = pl.BlockSpec(memory_space=pltpu.VMEM)
    far = pl.BlockSpec(memory_space=pltpu.HBM)

    if packed_form:
        sent = call(
            pack_kernel,
            "pack",
            PACK_MB,
            in_specs=[near, far, far],
            out_specs=far,
            out_shape=packed,
            scratch_shapes=[
                pltpu.VMEM(w_in.shape, BF16),
                pltpu.VMEM(cotangent.shape, BF16),
                pltpu.VMEM(packed.shape, BF16),
                pltpu.SemaphoreType.DMA((2 + peers // 2,)),
            ],
        )(token_ids.T, w_in, cotangent)
        arrived = (exchange(sent),)
    else:
        arrived = send_inputs(token_ids, w_in, cotangent, peers)

    taps = short_taps.reshape(3, 3, peers, chans)
    taps = lax.dynamic_index_in_dim(taps, lax.axis_index("tm"), axis=2, keepdims=False)
    filter_spec, entries, narrow, wide_tables = call(
        prepare_kernel,
        "prepare",
        32,
        in_specs=[pl.BlockSpec(memory_space=pltpu.SMEM)] + [near] * 9,
        out_shape=(
            shape(spec, F32),
            shape(embed_table.shape, BF16),
            shape((narrow_places(tables)[-1][1], 2 * LANES), BF16),
            shape((9 * chans + 2 * peers * GROUP, LANES), F32),
        ),
        cost_estimate=pl.CostEstimate(
            flops=10**10, bytes_accessed=3 * 10**7, transcendentals=0
        ),
    )(field_offsets, filters, embed_table, taps.reshape(3, 3 * chans, 1), *tables)
    if packed_form:
        out_shape = (shape(spec, BF16), packed)
        out_specs = (far, far)
        scratch_shapes = [pltpu.VMEM(packed.shape, BF16)] * 2
    else:
        out_shape = (
            shape(spec, BF16),
            shape(moved, BF16),
            shape((width, 3 * chans), BF16),
            shape((3, 3 * chans, 1), F32),
        )
        out_specs = (far, near, near, near)
        scratch_shapes = []
    operands = (entries, filter_spec, narrow, wide_tables)
    places = (entries, shape((3, 3 * chans, LANES), F32), filter_spec) + tables
    results = call(
        functools.partial(mixer_kernel, packed_form),
        "mixer",
        MIX_MB,
        in_specs=[far if packed_form else near] * len(arrived) + [far] * len(operands),
        out_shape=out_shape,
        out_specs=out_specs,
        scratch_shapes=[pltpu.VMEM(place.shape, place.dtype) for place in places]
        + [
            pltpu.SemaphoreType.DMA((len(narrow_places(tables)) + 8 + groups + 2 * QUARTERS,)),
            pltpu.VMEM(spec, BF16),
            pltpu.VMEM((embed_table.shape[0], steps), BF16),
            pltpu.VMEM(wide, BF16),
            pltpu.VMEM(wide, BF16),
            pltpu.VMEM(wide, BF16),
            pltpu.VMEM((3 * chans, steps), BF16),
        ]
        + scratch_shapes,
    )(*arrived, *operands)
    filter_grads = call(
        lagged_kernel,
        "lagged",
        24,
        out_shape=shape((2, chans, steps), F32),
        cost_estimate=pl.CostEstimate(
            flops=10**10, bytes_accessed=3 * 10**7, transcendentals=0
        ),
    )(results[0], *tables)
    if packed_form:
        mixer_out, weight_grads, tap_grads = call(
            unpack_kernel,
            "unpack",
            16,
            out_shape=(
                shape((tok_rows, width), BF16),
                shape((rows, 3 * width), F32),
                shape((3, 3 * width), F32),
            ),
        )(exchange(results[1]))
    else:
        mixer_out, weight_grads, tap_grads = send_results(*results[1:], peers, rows)
    return (mixer_out, weight_grads, tap_grads, filter_grads)


def solution(mesh):
    return jax.shard_map(
        local,
        mesh=mesh,
        in_specs=(
            P(("groups", "tm"), None),
            P("groups"),
            P(),
            P("tm", None),
            P(),
            P(None, "tm", None),
            P(("groups", "tm"), None),
        ),
        out_specs=(
            P(("groups", "tm"), None),
            P(("groups", "tm"), None),
            P("groups", None),
            P("groups", "tm", None),
        ),
        check_vma=False,
    )
```
